256 devices in a mesh: pb: 32 (over z, x), ha: 8 (over y, core).
Axes of the slice: x: 4, y: 4, z: 8, core: 2. Of those that a mesh axis runs over, the one named last changes fastest.
Arguments:
- queries: bfloat16 [4096, 4096], P('pb', 'ha')
- keys: bfloat16 [4096, 4096], P('pb', 'ha')
- values: bfloat16 [4096, 4096], P('pb', 'ha'), may hold values from -6 to 6
- theta: float32 [32, 6, 11], P('ha')
- mix: float32 [32, 4], P('ha')
- gain: float32 [4096], P('ha'), may hold values from 0.5 to 1.5
- out_weight: bfloat16 [4096, 4096], P('ha'), may hold values from -0.09375 to 0.09375
- turn_lengths: int32 [16], replicated, may hold values from 1 to 640, 4096 in all
Outputs:
- output: bfloat16 [4096, 4096], P('pb', 'ha')
The draws below stay inside these ranges and needn't reach their ends.
Inputs may be any that keep to these rules, and one draw needn't show every extreme that they name: `turn_lengths`: the turns' lengths sum to 4096; the longest turn has exactly 640 positions.
All inputs are finite; a program needn't handle non-finite values.
Results may differ from the reference program's by a relative error of at most 0.018.
Values may be sent and summed in bfloat16 or wider, within the bound.
A program may use at most 64 MiB of HBM per device.

```python
import math
import jax
import jax.numpy as jnp
import numpy as np
from jax import lax

D = 4096
HEADS = 32
DH = 128
GROUP = 4
QCONV = 6
KCONV = 11
TQ = 128
MAXBACK = 5
NT = 16
SEQ = 4096
MOST = 640
N_HA = 8


def query_key_pair(key):
    first_key = jax.random.fold_in(key, 101)
    second_key = jax.random.fold_in(key, 202)
    draw_shape = (SEQ, HEADS * DH)
    query_draw = jnp.clip(jax.random.normal(first_key, draw_shape, jnp.float32), -4.0, 4.0)
    key_draw = jnp.clip(jax.random.normal(second_key, draw_shape, jnp.float32), -4.0, 4.0)
    return (query_draw, key_draw)


def draw_queries(key, part):
    return query_key_pair(key)[0].astype(jnp.bfloat16)


def draw_keys(key, part):
    return query_key_pair(key)[1].astype(jnp.bfloat16)


def draw_theta(key, part):
    noise = jnp.clip(0.25 * jax.random.normal(jax.random.fold_in(key, 303), (HEADS, QCONV, KCONV), jnp.float32), -1.0, 1.0)
    query_tap = jnp.arange(QCONV, dtype=jnp.int32)[None, :, None]
    key_tap = jnp.arange(KCONV, dtype=jnp.int32)[None, None, :]
    center = ((query_tap == 0) & (key_tap == (KCONV - 1) // 2)).astype(jnp.float32)
    return noise + center


def draw_mix(key, part):
    noise = jnp.clip(0.3 * jax.random.normal(jax.random.fold_in(key, 404), (HEADS, GROUP), jnp.float32), -1.2, 1.2)
    head_num = jnp.arange(HEADS, dtype=jnp.int32)[:, None]
    member = jnp.arange(GROUP, dtype=jnp.int32)[None, :]
    return noise + (head_num % GROUP == member).astype(jnp.float32)


def shard_levels(key, extent, pieces, low, top_value):
    level, own = 1.0, jax.random.fold_in(key, 6)
    for position, blocks in pieces:
        steps = jnp.exp(jax.random.uniform(jax.random.fold_in(own, position), (blocks,), jnp.float32, low / len(pieces), top_value / len(pieces)))
        level = level * jnp.repeat(steps, extent[position] // blocks).reshape([-1 if axis == position else 1 for axis in range(len(extent))])
    return level


def split_up(number_of, total, most, slope):
    portions = [(1 << 20) // math.isqrt(standing ** slope) + 1 for standing in range(2, number_of + 1)]
    rest, given = total - most - (number_of - 1), [1] * (number_of - 1)
    while rest > 0:
        candidates = [i for i in range(number_of - 1) if given[i] < most]
        whole, budget = sum([portions[i] for i in candidates]), rest
        for i in candidates:
            more = min(most - given[i], max(1, budget * portions[i] // whole), rest)
            given[i] = given[i] + more
            rest = rest - more
    return np.array([most] + given)


def ragged_sizes(rng, amount, total, reach, skew):
    if amount == 2:
        one = jax.random.randint(rng, (), max(1, total - reach), min(reach, total - 1) + 1)
        return jnp.stack([one, total - one])
    tallies = jnp.asarray(split_up(amount, total, reach, skew), jnp.int32)
    pairs = (amount - 1) // 2
    donor, sink = tallies[1:1 + 2 * pairs:2], tallies[2:2 + 2 * pairs:2]
    slack = jnp.minimum(donor - 1, reach - sink)
    passed = jax.random.randint(jax.random.fold_in(rng, 1), (pairs,), 0, 1 << 20) % (slack + 1)
    tallies = tallies.at[1:1 + 2 * pairs:2].set(donor - passed).at[2:2 + 2 * pairs:2].set(sink + passed)
    return tallies[jax.random.permutation(jax.random.fold_in(rng, 2), amount)]


def scatter_about(own_key, shape, deviation, most, pieces=(), held_as=jnp.bfloat16):
    array = jax.random.normal(own_key, shape, jnp.float32) * deviation
    if len(pieces) > 0:
        array = shard_levels(own_key, shape, pieces, -0.22, 0.18) * array
    return jnp.clip(array, min=-most, max=most).astype(held_as)


def setup_inputs(seed: int = 0) -> dict:
    key_list = jax.random.split(jax.random.key(seed), 9)
    queries = draw_queries(jax.random.fold_in(key_list[8], 71), 0)
    keys = draw_keys(jax.random.fold_in(key_list[8], 71), 0)
    values = scatter_about(key_list[2], (SEQ, HEADS * DH), 1.0, 6.0, ((0, 32), (1, 8)))
    theta = draw_theta(jax.random.fold_in(key_list[8], 71), 0)
    mix = draw_mix(jax.random.fold_in(key_list[8], 71), 0)
    gain = jnp.clip(1.0 + 0.1 * jax.random.normal(key_list[5], (HEADS * DH,), jnp.float32), 0.5, 1.5)
    out_weight = scatter_about(key_list[6], (HEADS * DH, D), (HEADS * DH) ** -0.5, 0.09375, ((0, 8),))
    turn_lengths = ragged_sizes(key_list[7], NT, SEQ, MOST, 2).astype(jnp.int32)
    return {"queries": queries, "keys": keys, "values": values, "theta": theta, "mix": mix, "gain": gain, "out_weight": out_weight, "turn_lengths": turn_lengths}


def conv_block(scores, theta_part, row_pos, row_start, col_pos, out_cols):
    rim_rows = QCONV - 1
    count_rows = row_pos.shape[0]
    conv_sum = jnp.zeros((scores.shape[0], count_rows, out_cols), jnp.float32)
    above_start = col_pos[None, :] >= row_start[:, None]
    for offset_q in range(QCONV):
        allowed = above_start & (col_pos[None, :] <= row_pos[:, None] - offset_q)
        taken_rows = jnp.where(allowed[None], scores[:, rim_rows - offset_q:rim_rows - offset_q + count_rows, :], jnp.float32(0.0))
        for offset_k in range(KCONV):
            conv_sum = conv_sum + theta_part[:, offset_q, KCONV - 1 - offset_k][:, None, None] * taken_rows[:, :, offset_k:offset_k + out_cols]
    return conv_sum

def tile_group(query_ext, key_ext, val_ext, row_pos, row_start, key_base, theta_part, mix_part, gain_part):
    key_reach = (KCONV - 1) // 2
    win_cols = val_ext.shape[0]
    score_scale = 1.0 / math.sqrt(DH)
    scores = jnp.einsum('rhd,chd->hrc', query_ext.astype(jnp.float32), key_ext.astype(jnp.float32)) * score_scale
    col_pos = key_base - key_reach + jnp.arange(win_cols + 2 * key_reach, dtype=jnp.int32)
    conv_sum = conv_block(scores, theta_part, row_pos, row_start, col_pos, win_cols)
    key_pos = key_base + jnp.arange(win_cols, dtype=jnp.int32)
    keep_mask = (key_pos[None, :] >= row_start[:, None]) & (key_pos[None, :] <= row_pos[:, None])
    row_peak = lax.optimization_barrier(jnp.max(jnp.where(keep_mask[None], conv_sum, jnp.float32(-1e+30)), axis=-1))
    weights = jnp.where(keep_mask[None], jnp.exp(conv_sum - row_peak[..., None]), jnp.float32(0.0))
    row_total = lax.optimization_barrier(jnp.sum(weights, axis=-1))
    prob_bf = lax.optimization_barrier(weights.astype(jnp.bfloat16)).astype(jnp.float32)
    acc = jnp.einsum('pij,jc->pic', prob_bf, val_ext.astype(jnp.float32)) / row_total[..., None]
    acc = acc.reshape(GROUP, TQ, GROUP, DH)
    head_out = jnp.einsum('kp,pikd->ikd', mix_part, acc)
    mean_sq = lax.optimization_barrier(jnp.mean(head_out * head_out, axis=-1, keepdims=True))
    normed = head_out * lax.rsqrt(mean_sq + 1e-06) * gain_part.reshape(GROUP, DH)
    return normed.reshape(TQ, GROUP * DH).astype(jnp.bfloat16)

def reference(queries, keys, values, theta, mix, gain, out_weight, turn_lengths):
    rim_rows = QCONV - 1
    key_reach = (KCONV - 1) // 2
    win_cols = (MAXBACK + 1) * TQ
    seq_len = queries.shape[0]
    lengths = turn_lengths.astype(jnp.int32)
    starts = (jnp.cumsum(lengths) - lengths).astype(jnp.int32)
    positions = jnp.arange(seq_len, dtype=jnp.int32)
    row_start_all = lax.optimization_barrier(jnp.max(jnp.where(starts[None, :] <= positions[:, None], starts[None, :], 0), axis=1)).astype(jnp.int32)
    query_pad = jnp.pad(queries, ((rim_rows, 0), (0, 0)))
    key_pad = jnp.pad(keys, ((MAXBACK * TQ + key_reach, key_reach), (0, 0)))
    val_pad = jnp.pad(values, ((MAXBACK * TQ, 0), (0, 0)))
    head_cols = HEADS // N_HA * DH

    def one_tile(tile_num):
        first_row = (tile_num * TQ).astype(jnp.int32)
        query_tile = lax.dynamic_slice_in_dim(query_pad, first_row, TQ + rim_rows, 0).reshape(TQ + rim_rows, HEADS, DH)
        key_tile = lax.dynamic_slice_in_dim(key_pad, first_row, win_cols + 2 * key_reach, 0).reshape(win_cols + 2 * key_reach, HEADS, DH)
        val_tile = lax.dynamic_slice_in_dim(val_pad, first_row, win_cols, 0)
        row_pos = first_row + jnp.arange(TQ, dtype=jnp.int32)
        row_start = lax.dynamic_slice_in_dim(row_start_all, first_row, TQ, 0)
        key_base = first_row - MAXBACK * TQ

        def one_group(group_num):
            head_first = (group_num * GROUP).astype(jnp.int32)
            col_first = (group_num * GROUP * DH).astype(jnp.int32)
            return tile_group(lax.dynamic_slice_in_dim(query_tile, head_first, GROUP, 1), lax.dynamic_slice_in_dim(key_tile, head_first, GROUP, 1), lax.dynamic_slice_in_dim(val_tile, col_first, GROUP * DH, 1), row_pos, row_start, key_base, lax.dynamic_slice_in_dim(theta, head_first, GROUP, 0), lax.dynamic_slice_in_dim(mix, head_first, GROUP, 0), lax.dynamic_slice_in_dim(gain, col_first, GROUP * DH, 0))
        grouped = lax.map(one_group, jnp.arange(HEADS // GROUP, dtype=jnp.int32))
        normed = jnp.transpose(grouped, (1, 0, 2)).reshape(TQ, HEADS * DH)
        summed = jnp.zeros((TQ, out_weight.shape[1]), jnp.float32)
        for device_num in range(N_HA):
            lower = device_num * head_cols
            part_sum = jnp.dot(normed[:, lower:lower + head_cols], out_weight[lower:lower + head_cols], preferred_element_type=jnp.float32)
            summed = summed + lax.optimization_barrier(part_sum.astype(jnp.bfloat16)).astype(jnp.float32)
        return summed.astype(jnp.bfloat16)
    tiles = lax.map(one_tile, jnp.arange(seq_len // TQ, dtype=jnp.int32))
    return tiles.reshape(seq_len, out_weight.shape[1])
```

```python
import math

import jax
import jax.numpy as jnp
from jax import lax
from jax.sharding import PartitionSpec as P

GROUP = 4
QCONV = 6
KCONV = 11
MAXBACK = 5


def from_behind(block, axis, distance):
    devices = range(lax.axis_size(axis))
    route = [(i - distance, i) for i in devices if i - distance in devices]
    return lax.ppermute(block, axis, route)


def conv_block(scores, theta_part, row_pos, row_start, col_pos, out_cols):
    rim_rows = QCONV - 1
    count_rows = row_pos.shape[0]
    conv_sum = jnp.zeros((scores.shape[0], count_rows, out_cols), jnp.float32)
    above_start = col_pos[None, :] >= row_start[:, None]
    for offset_q in range(QCONV):
        allowed = above_start & (col_pos[None, :] <= row_pos[:, None] - offset_q)
        taken_rows = jnp.where(
            allowed[None],
            scores[:, rim_rows - offset_q : rim_rows - offset_q + count_rows, :],
            jnp.float32(0.0),
        )
        for offset_k in range(KCONV):
            conv_sum = (
                conv_sum
                + theta_part[:, offset_q, KCONV - 1 - offset_k][:, None, None]
                * taken_rows[:, :, offset_k : offset_k + out_cols]
            )
    return conv_sum


def per_device(queries, keys, values, theta, mix, gain, out_weight, turn_lengths):
    tile_rows = queries.shape[0]
    feature_cols = queries.shape[1]
    local_heads = theta.shape[0]
    head_size = feature_cols // local_heads
    groups = local_heads // GROUP
    group_cols = GROUP * head_size
    rim_rows = QCONV - 1
    key_reach = (KCONV - 1) // 2
    tile_index = lax.axis_index("pb")
    first_row = tile_index * tile_rows
    turn = jnp.arange(turn_lengths.shape[0], dtype=jnp.int32)
    starts = jnp.sum(jnp.where(turn[None, :] < turn[:, None], turn_lengths[None, :], 0), axis=1)
    row_pos = first_row + jnp.arange(tile_rows, dtype=jnp.int32)
    row_start = jnp.max(jnp.where(starts[None, :] <= row_pos[:, None], starts[None, :], 0), axis=1)
    earlier = from_behind(queries[tile_rows - rim_rows :], "pb", 1)
    query_ext = jnp.concatenate([earlier, queries], 0).reshape(
        tile_rows + rim_rows, local_heads, head_size
    )
    kv_pair = jnp.stack([keys, values], 0)
    blocks = [kv_pair[None]]
    for distance in range(1, MAXBACK + 1):
        blocks.insert(0, from_behind(kv_pair, "pb", distance)[None])
    window = jnp.concatenate(blocks, 0)
    key_span = (MAXBACK + 1) * tile_rows
    key_win = window[:, 0].reshape(key_span, feature_cols)
    val_win = window[:, 1].reshape(key_span, feature_cols)
    key_pad = jnp.pad(key_win, ((key_reach, key_reach), (0, 0))).reshape(
        key_span + 2 * key_reach, local_heads, head_size
    )
    key_base = first_row - MAXBACK * tile_rows
    score_scale = 1.0 / math.sqrt(head_size)
    state_carry = (
        jnp.full((local_heads, tile_rows), -1e30, jnp.float32),
        jnp.zeros((local_heads, tile_rows), jnp.float32),
        jnp.zeros((local_heads, tile_rows, group_cols), jnp.float32),
    )
    for block_num in range(MAXBACK + 1):
        block_row_peak, block_row_total, block_accumulated = state_carry
        lower = block_num * tile_rows
        key_slice = key_pad[lower : lower + tile_rows + 2 * key_reach]
        scores = (
            jnp.einsum("rhd,chd->hrc", query_ext, key_slice, preferred_element_type=jnp.float32)
            * score_scale
        )
        col_pos = (
            key_base + lower - key_reach + jnp.arange(tile_rows + 2 * key_reach, dtype=jnp.int32)
        )
        conv_sum = conv_block(scores, theta, row_pos, row_start, col_pos, tile_rows)
        key_pos = key_base + lower + jnp.arange(tile_rows, dtype=jnp.int32)
        keep_mask = (key_pos[None, :] >= row_start[:, None]) & (
            key_pos[None, :] <= row_pos[:, None]
        )
        masked = jnp.where(keep_mask[None], conv_sum, jnp.float32(-1e30))
        new_peak = jnp.maximum(block_row_peak, jnp.max(masked, axis=-1))
        weights = jnp.where(
            keep_mask[None], jnp.exp(conv_sum - new_peak[..., None]), jnp.float32(0.0)
        )
        factor = jnp.exp(block_row_peak - new_peak)
        new_total = block_row_total * factor + jnp.sum(weights, axis=-1)
        prob_bf = weights.astype(jnp.bfloat16).reshape(groups, GROUP, tile_rows, tile_rows)
        val_block = val_win[lower : lower + tile_rows].reshape(tile_rows, groups, group_cols)
        update = jnp.einsum(
            "gpij,jgc->gpic", prob_bf, val_block, preferred_element_type=jnp.float32
        )
        update = update.reshape(local_heads, tile_rows, group_cols)
        state_carry = (new_peak, new_total, block_accumulated * factor[..., None] + update)
    row_peak, row_total, accumulated = state_carry
    normalized = (accumulated / row_total[..., None]).reshape(
        groups, GROUP, tile_rows, GROUP, head_size
    )
    mix_grid = mix.reshape(groups, GROUP, GROUP)
    head_out = jnp.einsum("gkp,gpikd->gikd", mix_grid, normalized)
    head_out = jnp.transpose(head_out, (1, 0, 2, 3)).reshape(tile_rows, local_heads, head_size)
    mean_sq = jnp.mean(head_out * head_out, axis=-1, keepdims=True)
    normed = (
        (head_out * lax.rsqrt(mean_sq + 1e-06) * gain.reshape(local_heads, head_size))
        .reshape(tile_rows, feature_cols)
        .astype(jnp.bfloat16)
    )
    summed = lax.psum_scatter(
        lax.dot_general(
            out_weight, normed, (((0,), (1,)), ((), ())), preferred_element_type=jnp.float32
        ).astype(jnp.bfloat16),
        "ha",
        scatter_dimension=0,
        tiled=True,
    ).astype(jnp.float32)
    return summed.T.astype(jnp.bfloat16)


def solution(mesh):
    return jax.shard_map(
        per_device,
        mesh=mesh,
        in_specs=(
            P("pb", "ha"),
            P("pb", "ha"),
            P("pb", "ha"),
            P("ha", None, None),
            P("ha", None),
            P("ha"),
            P("ha", None),
            P(),
        ),
        out_specs=P("pb", "ha"),
        check_vma=False,
    )
```

```python
import functools
import math

import jax
import jax.numpy as jnp
from jax import lax
from jax.experimental import pallas as pl
from jax.experimental.pallas import tpu as pltpu
from jax.sharding import PartitionSpec as P

GROUP = 4
QCONV = 6
KCONV = 11
REACH = (KCONV - 1) // 2
MAXBACK = 5
ROWS = 128
DH = 128
COLS = GROUP * DH
RING_X = 4
CORES = 2
PAD = 16
STEP = 112
WINDOWS = 7
SPAN = PAD + (MAXBACK + 1) * ROWS + PAD
QROWS = PAD + ROWS
HALF = ROWS // 2
MESH = pl.DeviceIdType.MESH
Z_OWN, X_ONE, X_THREE, X_TWO, Z_FIVE = range(5)


def slot_row(distance):
    return PAD + (MAXBACK - distance) * ROWS


def kernel(
    pb_size,
    ha_size,
    turns_ref,
    q_hbm,
    k_hbm,
    v_hbm,
    theta_ref,
    mix_ref,
    gain_ref,
    w_hbm,
    out_ref,
    qext,
    kwin,
    vwin,
    w_vmem,
    taps,
    band,
    row_lo,
    row_hi,
    row_ok,
    shifted,
    lhs,
    conv_buf,
    probs,
    inv_total,
    vext,
    acc,
    normed,
    core_out,
    core_in,
    chip_out,
    chip_in,
    load_sem,
    tail_sem,
    send_sem,
    recv_sem,
    core_send,
    core_recv,
    chip_send,
    chip_recv,
):
    pb = lax.axis_index("pb")
    ha = lax.axis_index("ha")
    ring_z = pb_size // RING_X
    ring_y = ha_size // CORES
    x, z = pb % RING_X, pb // RING_X
    core, y = ha % CORES, ha // CORES

    def at(new_z, new_x):
        return ((new_z % ring_z) * RING_X + new_x % RING_X, ha)

    x_next, x_back = at(z, x + 1), at(z, x + RING_X - 1)
    z_next, z_back = at(z + 1, x), at(z + ring_z - 1, x)
    pb_next, pb_back = ((pb + 1) % pb_size, ha), ((pb + pb_size - 1) % pb_size, ha)
    twin = (pb, y * CORES + 1 - core)

    def chip(k):
        return (pb, ((y + k) % ring_y) * CORES + core)

    own = slot_row(0)
    loads = [
        pltpu.make_async_copy(k_hbm, kwin.at[pl.ds(own, ROWS)], load_sem.at[0]),
        pltpu.make_async_copy(v_hbm, vwin.at[pl.ds(own, ROWS)], load_sem.at[1]),
        pltpu.make_async_copy(q_hbm, qext.at[pl.ds(PAD, ROWS)], load_sem.at[2]),
        pltpu.make_async_copy(w_hbm, w_vmem, load_sem.at[3]),
    ]
    for load in loads:
        load.start()

    barrier = pltpu.get_barrier_semaphore()
    greeted = [x_next, x_back, z_next, z_back, pb_next, pb_back, twin]
    greeted += [chip(k) for k in range(1, ring_y)]
    for other in greeted:
        pl.semaphore_signal(barrier, inc=1, device_id=other, device_id_type=MESH)
    pl.semaphore_wait(barrier, len(greeted))

    def message(kind, chunk):
        win = kwin if chunk < 2 else vwin
        shift = (chunk % 2) * HALF
        last = x == RING_X - 1
        src, dst, target = {
            Z_OWN: (own, slot_row(4), z_next),
            X_ONE: (jnp.where(last, slot_row(4), own), slot_row(1), x_next),
            X_THREE: (jnp.where(x == 0, own, slot_row(4)), slot_row(3), x_back),
            X_TWO: (jnp.where(last, slot_row(5), slot_row(1)), slot_row(2), x_next),
            Z_FIVE: (slot_row(1), slot_row(5), z_next),
        }[kind]
        return pltpu.make_async_remote_copy(
            src_ref=win.at[pl.ds(pl.multiple_of(src + shift, 16), HALF)],
            dst_ref=win.at[pl.ds(dst + shift, HALF)],
            send_sem=send_sem.at[kind, chunk],
            recv_sem=recv_sem.at[kind, chunk],
            device_id=target,
            device_id_type=MESH,
        )

    tail = pltpu.make_async_remote_copy(
        src_ref=qext.at[pl.ds(ROWS, PAD)],
        dst_ref=qext.at[pl.ds(0, PAD)],
        send_sem=tail_sem.at[0],
        recv_sem=tail_sem.at[1],
        device_id=pb_next,
        device_id_type=MESH,
    )

    def first(chunk):
        message(Z_OWN, chunk).start()

        @pl.when(x < RING_X - 1)
        def _():
            message(X_ONE, chunk).start()

        @pl.when(x == 0)
        def _():
            message(X_THREE, chunk).start()

    def after_four(chunk):
        message(Z_OWN, chunk).wait_recv()

        @pl.when(x == RING_X - 1)
        def _():
            message(X_ONE, chunk).start()

        @pl.when(x > 0)
        def _():
            message(X_THREE, chunk).start()

    def after_one(chunk):
        message(X_ONE, chunk).wait_recv()
        message(Z_FIVE, chunk).start()

        @pl.when(x < RING_X - 1)
        def _():
            message(X_TWO, chunk).start()

    def after_five(chunk):
        message(Z_FIVE, chunk).wait_recv()

        @pl.when(x == RING_X - 1)
        def _():
            message(X_TWO, chunk).start()

    def last_two(chunk):
        message(X_TWO, chunk).wait_recv()
        message(X_THREE, chunk).wait_recv()

    loads[0].wait()
    first(0)
    first(1)
    loads[2].wait()
    tail.start()

    first_row = pb * ROWS
    for win in (kwin, vwin):
        win[0:PAD] = jnp.zeros((PAD, COLS), jnp.bfloat16)
        win[SPAN - PAD : SPAN] = jnp.zeros((PAD, COLS), jnp.bfloat16)
    pos = first_row - PAD + lax.broadcasted_iota(jnp.int32, (QROWS, DH), 0)
    row_start = jnp.zeros((QROWS, DH), jnp.int32)
    start = jnp.int32(0)
    for n in range(turns_ref.shape[0]):
        row_start = jnp.where(pos >= start, start, row_start)
        start = start + turns_ref[n]
    key_zero = first_row - slot_row(0)
    row_lo[...] = row_start - key_zero
    row_hi[...] = pos - key_zero
    rel = (pos - row_start)[PAD:]
    for a in range(QCONV):
        row_ok[a] = jnp.where(rel >= a, 1.0, 0.0).astype(jnp.bfloat16)
    taps[...] = jnp.zeros(taps.shape, jnp.float32)
    scaled_theta = theta_ref[...] * (1.0 / math.sqrt(DH))
    taps[:, 0:QCONV, 0 : REACH + 1] = scaled_theta[:, :, REACH:]
    taps[:, 0:QCONV, DH - REACH : DH] = scaled_theta[:, :, :REACH]

    after_four(0)
    after_four(1)
    loads[1].wait()

    def make_band(h, carry):
        for a in range(QCONV):
            line = jnp.broadcast_to(taps[h, a : a + 1, :], (DH, DH))
            square = pltpu.roll(line, 0, 1, stride=1, stride_axis=0)
            band[h, a * DH : (a + 1) * DH, :] = square.astype(jnp.bfloat16)
        return carry

    lax.fori_loop(0, 2, make_band, 0)
    after_one(0)
    after_one(1)
    first(2)
    first(3)
    lax.fori_loop(2, 4, make_band, 0)
    after_five(0)
    after_five(1)
    tail.wait_recv()
    last_two(0)
    last_two(1)

    lane = lax.broadcasted_iota(jnp.int32, (ROWS, DH), 1)
    q_lane = lax.broadcasted_iota(jnp.int32, (QROWS, DH), 1)
    inner = (lane >= 8) & (lane < 8 + STEP)

    def head(h, carry):
        cols = pl.ds(pl.multiple_of(h * DH, DH), DH)
        q_head = qext[:, cols]
        for t in range(WINDOWS):
            k_head = kwin[t * STEP : t * STEP + DH, cols]
            scores = lax.dot_general(
                q_head, k_head, (((1,), (1,)), ((), ())), preferred_element_type=jnp.float32
            )
            place = q_lane + t * STEP
            seen = (place >= row_lo[...]) & (place <= row_hi[...])
            shifted[t] = jnp.where(seen, scores, 0.0)
        for t in range(WINDOWS):
            for a in range(QCONV):
                moved = shifted[t, PAD - a : PAD - a + ROWS, :].astype(jnp.bfloat16)
                lhs[t * ROWS : (t + 1) * ROWS, a * DH : (a + 1) * DH] = moved * row_ok[a]
        conv = jnp.dot(lhs[...], band[h], preferred_element_type=jnp.float32)
        peak = jnp.full((ROWS, DH), -1e30, jnp.float32)
        lo, hi = row_lo[PAD:], row_hi[PAD:]
        for t in range(WINDOWS):
            place = lane + t * STEP
            kept = (place >= lo) & (place <= hi) & inner
            masked = jnp.where(kept, conv[t * ROWS : (t + 1) * ROWS], -1e30)
            conv_buf[t] = masked
            peak = jnp.maximum(peak, masked)
        peak = jnp.max(peak, axis=1, keepdims=True)
        total = jnp.zeros((ROWS, DH), jnp.float32)
        rows = pl.ds(pl.multiple_of(h * ROWS, ROWS), ROWS)
        for t in range(WINDOWS):
            weights = jnp.exp(conv_buf[t] - peak)
            total = total + weights
            probs[rows, t * DH : (t + 1) * DH] = weights.astype(jnp.bfloat16)
        total = jnp.sum(total, axis=1, keepdims=True)
        inv_total[h] = jnp.broadcast_to(1.0 / total, (ROWS, DH))

        @pl.when(h == 0)
        def _():
            after_four(2)
            after_four(3)

        @pl.when(h == 1)
        def _():
            after_one(2)
            after_one(3)

        @pl.when(h == 2)
        def _():
            after_five(2)
            after_five(3)

        return carry

    lax.fori_loop(0, GROUP, head, 0)
    last_two(2)
    last_two(3)
    for t in range(WINDOWS):
        vext[t * DH : (t + 1) * DH] = vwin[t * STEP : t * STEP + DH]

    def mix_values(p, carry):
        rows = pl.ds(pl.multiple_of(p * ROWS, ROWS), ROWS)
        acc[rows] = jnp.dot(probs[rows], vext[...], preferred_element_type=jnp.float32)
        return carry

    lax.fori_loop(0, GROUP, mix_values, 0)
    for h in range(GROUP):
        attn = jnp.zeros((ROWS, DH), jnp.float32)
        for p in range(GROUP):
            piece = acc[p * ROWS : (p + 1) * ROWS, h * DH : (h + 1) * DH] * inv_total[p]
            attn = attn + mix_ref[h, p] * piece
        mean_sq = jnp.mean(attn * attn, axis=1, keepdims=True)
        scaled = attn * lax.rsqrt(mean_sq + 1e-06) * gain_ref[:, h * DH : (h + 1) * DH]
        normed[:, h * DH : (h + 1) * DH] = scaled.astype(jnp.bfloat16)

    loads[3].wait()

    def partial(k, side):
        group = ((y + k) % ring_y) * CORES + side
        cols = pl.ds(pl.multiple_of(group * COLS, COLS), COLS)
        return jnp.dot(normed[...], w_vmem[:, cols], preferred_element_type=jnp.float32)

    def to_twin(k):
        return pltpu.make_async_remote_copy(
            src_ref=core_out.at[k],
            dst_ref=core_in.at[k],
            send_sem=core_send.at[k],
            recv_sem=core_recv.at[k],
            device_id=twin,
            device_id_type=MESH,
        )

    def to_chip(k):
        return pltpu.make_async_remote_copy(
            src_ref=chip_out.at[k - 1],
            dst_ref=chip_in.at[k - 1],
            send_sem=chip_send.at[k - 1],
            recv_sem=chip_recv.at[k - 1],
            device_id=chip(k),
            device_id_type=MESH,
        )

    order = [2, 1, 3, 0] if ring_y == 4 else list(range(ring_y - 1, -1, -1))
    for k in order:
        core_out[k] = partial(k, 1 - core).astype(jnp.bfloat16)
        to_twin(k).start()
    for k in order:
        mine = partial(k, core).astype(jnp.bfloat16).astype(jnp.float32)
        to_twin(k).wait_recv()
        both = mine + core_in[k].astype(jnp.float32)
        if k:
            chip_out[k - 1] = both.astype(jnp.bfloat16)
            to_chip(k).start()
        else:
            acc[0:ROWS] = both
    result = acc[0:ROWS]
    for k in sorted(order[:-1], key=lambda k: k == 2):
        to_chip(k).wait_recv()
        result = result + chip_in[k - 1].astype(jnp.float32)
    out_ref[...] = result.astype(jnp.bfloat16)

    tail.wait_send()
    for kind in range(5):
        for chunk in range(4):
            message(kind, chunk).wait_send()
    for k in order:
        to_twin(k).wait_send()
        if k:
            to_chip(k).wait_send()


def solution(mesh):
    pb_size, ha_size = mesh.shape["pb"], mesh.shape["ha"]
    ring_y = ha_size // CORES
    bf16, f32 = jnp.bfloat16, jnp.float32

    def per_device(queries, keys, values, theta, mix, gain, out_weight, turn_lengths):
        hbm = pl.BlockSpec(memory_space=pl.ANY)
        vmem = pl.BlockSpec(memory_space=pltpu.VMEM)
        smem = pl.BlockSpec(memory_space=pltpu.SMEM)
        far = max(ring_y - 1, 1)
        return pl.pallas_call(
            functools.partial(kernel, pb_size, ha_size),
            out_shape=jax.ShapeDtypeStruct((ROWS, COLS), bf16),
            in_specs=[smem, hbm, hbm, hbm, vmem, smem, vmem, hbm],
            out_specs=vmem,
            scratch_shapes=[
                pltpu.VMEM((QROWS, COLS), bf16),
                pltpu.VMEM((SPAN, COLS), bf16),
                pltpu.VMEM((SPAN, COLS), bf16),
                pltpu.VMEM(out_weight.shape, bf16),
                pltpu.VMEM((GROUP, 8, DH), f32),
                pltpu.VMEM((GROUP, QCONV * DH, DH), bf16),
                pltpu.VMEM((QROWS, DH), jnp.int32),
                pltpu.VMEM((QROWS, DH), jnp.int32),
                pltpu.VMEM((QCONV, ROWS, DH), bf16),
                pltpu.VMEM((WINDOWS, QROWS, DH), f32),
                pltpu.VMEM((WINDOWS * ROWS, QCONV * DH), bf16),
                pltpu.VMEM((WINDOWS, ROWS, DH), f32),
                pltpu.VMEM((GROUP * ROWS, WINDOWS * DH), bf16),
                pltpu.VMEM((GROUP, ROWS, DH), f32),
                pltpu.VMEM((WINDOWS * DH, COLS), bf16),
                pltpu.VMEM((GROUP * ROWS, COLS), f32),
                pltpu.VMEM((ROWS, COLS), bf16),
                pltpu.VMEM((ring_y, ROWS, COLS), bf16),
                pltpu.VMEM((ring_y, ROWS, COLS), bf16),
                pltpu.VMEM((far, ROWS, COLS), bf16),
                pltpu.VMEM((far, ROWS, COLS), bf16),
                pltpu.SemaphoreType.DMA((4,)),
                pltpu.SemaphoreType.DMA((2,)),
                pltpu.SemaphoreType.DMA((5, 4)),
                pltpu.SemaphoreType.DMA((5, 4)),
                pltpu.SemaphoreType.DMA((ring_y,)),
                pltpu.SemaphoreType.DMA((ring_y,)),
                pltpu.SemaphoreType.DMA((far,)),
                pltpu.SemaphoreType.DMA((far,)),
            ],
            compiler_params=pltpu.CompilerParams(
                collective_id=0, has_side_effects=True, vmem_limit_bytes=48 * 1024 * 1024
            ),
        )(turn_lengths, queries, keys, values, theta, mix, gain.reshape(1, COLS), out_weight)

    return jax.shard_map(
        per_device,
        mesh=mesh,
        in_specs=(
            P("pb", "ha"),
            P("pb", "ha"),
            P("pb", "ha"),
            P("ha", None, None),
            P("ha", None),
            P("ha"),
            P("ha", None),
            P(),
        ),
        out_specs=P("pb", "ha"),
        check_vma=False,
    )
```

```python
import functools
import math

import jax
import jax.numpy as jnp
from jax import lax
from jax.experimental import pallas as pl
from jax.experimental.pallas import tpu as pltpu
from jax.sharding import PartitionSpec as P

GROUP = 4
QCONV = 6
KCONV = 11
REACH = (KCONV - 1) // 2
MAXBACK = 5
ROWS = 128
DH = 128
COLS = GROUP * DH
RING_X = 4
CORES = 2
PAD = 16
STEP = 112
WINDOWS = 7
SPAN = PAD + (MAXBACK + 1) * ROWS + PAD
QROWS = PAD + ROWS
HALF = ROWS // 2
MESH = pl.DeviceIdType.MESH
FOUR, ONE, TWO, THREE, FIVE = range(5)
FAR = 2


def slot_row(distance):
    return PAD + (MAXBACK - distance) * ROWS


def kernel(
    pb_size,
    ha_size,
    turns_hbm,
    q_hbm,
    k_hbm,
    v_hbm,
    theta_hbm,
    mix_hbm,
    gain_hbm,
    w_hbm,
    out_ref,
    turns_ref,
    theta_ref,
    mix_ref,
    gain_ref,
    qext,
    kwin,
    vwin,
    w_vmem,
    taps,
    band,
    row_lo,
    row_hi,
    row_ok,
    shifted,
    lhs,
    conv_buf,
    probs,
    inv_total,
    vext,
    acc,
    normed,
    core_out,
    core_in,
    chip_out,
    chip_in,
    q_behind,
    load_sem,
    tail_send,
    tail_recv,
    send_sem,
    recv_sem,
    core_send,
    core_recv,
    chip_send,
    chip_recv,
):
    pb = lax.axis_index("pb")
    ha = lax.axis_index("ha")
    ring_z = pb_size // RING_X
    ring_y = ha_size // CORES
    x, z = pb % RING_X, pb // RING_X
    core, y = ha % CORES, ha // CORES

    def at(new_z, new_x):
        return ((new_z % ring_z) * RING_X + new_x % RING_X, ha)

    x_next, x_over, x_back = at(z, x + 1), at(z, x + 2), at(z, x + RING_X - 1)
    z_next, z_back = at(z + 1, x), at(z + ring_z - 1, x)
    twin = (pb, y * CORES + 1 - core)

    def chip(k):
        return (pb, ((y + k) % ring_y) * CORES + core)

    own = slot_row(0)
    loads = [
        pltpu.make_async_copy(k_hbm, kwin.at[pl.ds(own, ROWS)], load_sem.at[0]),
        pltpu.make_async_copy(v_hbm, vwin.at[pl.ds(own, ROWS)], load_sem.at[1]),
        pltpu.make_async_copy(q_hbm, qext.at[pl.ds(PAD, ROWS)], load_sem.at[2]),
        pltpu.make_async_copy(turns_hbm, turns_ref, load_sem.at[4]),
        pltpu.make_async_copy(theta_hbm, theta_ref, load_sem.at[5]),
        pltpu.make_async_copy(mix_hbm, mix_ref, load_sem.at[6]),
        pltpu.make_async_copy(gain_hbm, gain_ref, load_sem.at[7]),
        pltpu.make_async_copy(w_hbm, w_vmem, load_sem.at[3]),
    ]
    for load in loads:
        load.start()

    barrier = pltpu.get_barrier_semaphore()
    greeted = [x_next, x_over, x_back, z_next, z_back, twin]
    greeted += [chip(k) for k in range(1, ring_y)]
    for other in greeted:
        pl.semaphore_signal(barrier, inc=1, device_id=other, device_id_type=MESH)
    pl.semaphore_wait(barrier, len(greeted))

    def message(kind, chunk):
        win = kwin if chunk < 2 else vwin
        shift = (chunk % 2) * HALF
        behind = slot_row(4)
        src, dst, target = {
            FOUR: (own, slot_row(4), z_next),
            ONE: (jnp.where(x < 3, own, behind), slot_row(1), x_next),
            TWO: (jnp.where(x < 2, own, behind), slot_row(2), x_over),
            THREE: (jnp.where(x < 1, own, behind), slot_row(3), x_back),
            FIVE: (slot_row(1), slot_row(5), z_next),
        }[kind]
        return pltpu.make_async_remote_copy(
            src_ref=win.at[pl.ds(pl.multiple_of(src + shift, 16), HALF)],
            dst_ref=win.at[pl.ds(dst + shift, HALF)],
            send_sem=send_sem.at[kind, chunk],
            recv_sem=recv_sem.at[kind, chunk],
            device_id=target,
            device_id_type=MESH,
        )

    def tail_copy(src, dst, n, target):
        return pltpu.make_async_remote_copy(
            src_ref=src,
            dst_ref=dst,
            send_sem=tail_send.at[n],
            recv_sem=tail_recv.at[n],
            device_id=target,
            device_id_type=MESH,
        )

    tail_z = tail_copy(qext.at[pl.ds(ROWS, PAD)], q_behind, 0, z_next)
    tail_own = tail_copy(qext.at[pl.ds(ROWS, PAD)], qext.at[pl.ds(0, PAD)], 1, x_next)
    tail_behind = tail_copy(q_behind, qext.at[pl.ds(0, PAD)], 1, x_next)

    def from_own(chunk):
        for kind, bound in ((ONE, 3), (TWO, 2), (THREE, 1)):

            @pl.when(x < bound)
            def _(kind=kind):
                message(kind, chunk).start()

    def from_behind(chunk):
        message(FOUR, chunk).wait_recv()
        for kind, bound in ((ONE, 3), (TWO, 2), (THREE, 1)):

            @pl.when(x >= bound)
            def _(kind=kind):
                message(kind, chunk).start()

    def to_five(chunk):
        message(ONE, chunk).wait_recv()
        message(FIVE, chunk).start()

    loads[0].wait()
    for chunk in (0, 1):
        message(FOUR, chunk).start()
        from_own(chunk)
    loads[2].wait()
    tail_z.start()

    @pl.when(x < 3)
    def _():
        tail_own.start()

    loads[1].wait()
    for chunk in (2, 3):
        message(FOUR, chunk).start()
    loads[3].wait()
    loads[4].wait()
    first_row = pb * ROWS
    for win in (kwin, vwin):
        win[0:PAD] = jnp.zeros((PAD, COLS), jnp.bfloat16)
        win[SPAN - PAD : SPAN] = jnp.zeros((PAD, COLS), jnp.bfloat16)
    pos = first_row - PAD + lax.broadcasted_iota(jnp.int32, (QROWS, DH), 0)
    row_start = jnp.zeros((QROWS, DH), jnp.int32)
    start = jnp.int32(0)
    for n in range(turns_ref.shape[0]):
        row_start = jnp.where(pos >= start, start, row_start)
        start = start + turns_ref[n]
    key_zero = first_row - slot_row(0)
    row_lo[...] = row_start - key_zero
    row_hi[...] = pos - key_zero
    rel = (pos - row_start)[PAD:]
    for a in range(QCONV):
        row_ok[a] = jnp.where(rel >= a, 1.0, 0.0).astype(jnp.bfloat16)
    taps[...] = jnp.zeros(taps.shape, jnp.float32)
    scaled_theta = theta_ref[...] * (1.0 / math.sqrt(DH))
    taps[:, 0:GROUP, 0 : REACH + 1] = scaled_theta[:, :, REACH:]
    taps[:, 0:GROUP, DH - REACH : DH] = scaled_theta[:, :, :REACH]

    for chunk in (0, 1):
        from_behind(chunk)
    tail_z.wait_recv()

    @pl.when(x == 3)
    def _():
        tail_behind.start()

    for chunk in (2, 3):
        from_own(chunk)

    def make_band(h, carry):
        for a in range(QCONV):
            line = jnp.broadcast_to(taps[a, pl.ds(h, 1), :], (DH, DH))
            square = pltpu.roll(line, 0, 1, stride=1, stride_axis=0)
            band[h, a * DH : (a + 1) * DH, :] = square.astype(jnp.bfloat16)
        return carry

    lax.fori_loop(0, GROUP, make_band, 0)
    to_five(0)
    to_five(1)
    from_behind(2)
    from_behind(3)
    tail_own.wait_recv()
    for chunk in (0, 1):
        message(TWO, chunk).wait_recv()
        message(THREE, chunk).wait_recv()

    lane = lax.broadcasted_iota(jnp.int32, (ROWS, DH), 1)
    q_lane = lax.broadcasted_iota(jnp.int32, (QROWS, DH), 1)
    inner = (lane >= 8) & (lane < 8 + STEP)

    def convolve(h, windows):
        cols = pl.ds(pl.multiple_of(h * DH, DH), DH)
        q_head = qext[:, cols]
        for t in windows:
            k_head = kwin[t * STEP : t * STEP + DH, cols]
            scores = lax.dot_general(
                q_head, k_head, (((1,), (1,)), ((), ())), preferred_element_type=jnp.float32
            )
            place = q_lane + t * STEP
            seen = (place >= row_lo[...]) & (place <= row_hi[...])
            shifted[t] = jnp.where(seen, scores, 0.0)
        for t in windows:
            for a in range(QCONV):
                moved = shifted[t, PAD - a : PAD - a + ROWS, :].astype(jnp.bfloat16)
                lhs[t * ROWS : (t + 1) * ROWS, a * DH : (a + 1) * DH] = moved * row_ok[a]
        top, end = windows[0], windows[-1] + 1
        conv = jnp.dot(
            lhs[top * ROWS : end * ROWS], band[h], preferred_element_type=jnp.float32
        )
        lo, hi = row_lo[PAD:], row_hi[PAD:]
        for t in windows:
            place = lane + t * STEP
            kept = (place >= lo) & (place <= hi) & inner
            piece = conv[(t - top) * ROWS : (t - top + 1) * ROWS]
            conv_buf[h, t] = jnp.where(kept, piece, -1e30)

    near, far = list(range(FAR, WINDOWS)), list(range(FAR))

    def near_head(h, carry):
        convolve(h, near)
        for when, chunk in ((1, 2), (2, 3)):

            @pl.when((h == when) & (x > 0))
            def _(chunk=chunk):
                to_five(chunk)

        return carry

    lax.fori_loop(0, GROUP, near_head, 0)

    @pl.when(x == 0)
    def _():
        to_five(2)
        to_five(3)

    for chunk in (0, 1):
        message(FIVE, chunk).wait_recv()

    def far_head(h, carry):
        convolve(h, far)
        peak = conv_buf[h, 0]
        for t in range(1, WINDOWS):
            peak = jnp.maximum(peak, conv_buf[h, t])
        peak = jnp.max(peak, axis=1, keepdims=True)
        total = jnp.zeros((ROWS, DH), jnp.float32)
        rows = pl.ds(pl.multiple_of(h * ROWS, ROWS), ROWS)
        for t in range(WINDOWS):
            weights = jnp.exp(conv_buf[h, t] - peak)
            total = total + weights
            probs[rows, t * DH : (t + 1) * DH] = weights.astype(jnp.bfloat16)
        total = jnp.sum(total, axis=1, keepdims=True)
        inv_total[h] = jnp.broadcast_to(1.0 / total, (ROWS, DH))
        return carry

    lax.fori_loop(0, GROUP, far_head, 0)
    split = FAR * DH
    for chunk in (2, 3):
        message(TWO, chunk).wait_recv()
        message(THREE, chunk).wait_recv()
    for t in near:
        vext[t * DH : (t + 1) * DH] = vwin[t * STEP : t * STEP + DH]

    def near_values(p, carry):
        rows = pl.ds(pl.multiple_of(p * ROWS, ROWS), ROWS)
        acc[rows] = jnp.dot(
            probs[rows, split:], vext[split:], preferred_element_type=jnp.float32
        )
        return carry

    lax.fori_loop(0, GROUP, near_values, 0)
    for chunk in (2, 3):
        message(FIVE, chunk).wait_recv()
    for t in far:
        vext[t * DH : (t + 1) * DH] = vwin[t * STEP : t * STEP + DH]

    def far_values(p, carry):
        rows = pl.ds(pl.multiple_of(p * ROWS, ROWS), ROWS)
        acc[rows] += jnp.dot(
            probs[rows, :split], vext[:split], preferred_element_type=jnp.float32
        )
        return carry

    lax.fori_loop(0, GROUP, far_values, 0)
    for load in loads[5:]:
        load.wait()
    for h in range(GROUP):
        attn = jnp.zeros((ROWS, DH), jnp.float32)
        for p in range(GROUP):
            piece = acc[p * ROWS : (p + 1) * ROWS, h * DH : (h + 1) * DH] * inv_total[p]
            attn = attn + mix_ref[h, p] * piece
        mean_sq = jnp.mean(attn * attn, axis=1, keepdims=True)
        scaled = attn * lax.rsqrt(mean_sq + 1e-06) * gain_ref[:, h * DH : (h + 1) * DH]
        normed[:, h * DH : (h + 1) * DH] = scaled.astype(jnp.bfloat16)

    def partial(k, side):
        group = ((y + k) % ring_y) * CORES + side
        cols = pl.ds(pl.multiple_of(group * COLS, COLS), COLS)
        return jnp.dot(normed[...], w_vmem[:, cols], preferred_element_type=jnp.float32)

    def to_twin(k):
        return pltpu.make_async_remote_copy(
            src_ref=core_out.at[k],
            dst_ref=core_in.at[k],
            send_sem=core_send.at[k],
            recv_sem=core_recv.at[k],
            device_id=twin,
            device_id_type=MESH,
        )

    def to_chip(k):
        return pltpu.make_async_remote_copy(
            src_ref=chip_out.at[k - 1],
            dst_ref=chip_in.at[k - 1],
            send_sem=chip_send.at[k - 1],
            recv_sem=chip_recv.at[k - 1],
            device_id=chip(k),
            device_id_type=MESH,
        )

    order = [2, 1, 3, 0] if ring_y == 4 else list(range(ring_y - 1, -1, -1))
    for k in order:
        core_out[k] = partial(k, 1 - core).astype(jnp.bfloat16)
        to_twin(k).start()
    for k in order:
        mine = partial(k, core).astype(jnp.bfloat16).astype(jnp.float32)
        to_twin(k).wait_recv()
        both = mine + core_in[k].astype(jnp.float32)
        if k:
            chip_out[k - 1] = both.astype(jnp.bfloat16)
            to_chip(k).start()
        else:
            acc[0:ROWS] = both
    result = acc[0:ROWS]
    for k in sorted(order[:-1], key=lambda k: k == 2):
        to_chip(k).wait_recv()
        result = result + chip_in[k - 1].astype(jnp.float32)
    out_ref[...] = result.astype(jnp.bfloat16)

    tail_z.wait_send()
    tail_own.wait_send()
    for kind in range(5):
        for chunk in range(4):
            message(kind, chunk).wait_send()
    for k in order:
        to_twin(k).wait_send()
        if k:
            to_chip(k).wait_send()


def solution(mesh):
    pb_size, ha_size = mesh.shape["pb"], mesh.shape["ha"]
    ring_y = ha_size // CORES
    bf16, f32 = jnp.bfloat16, jnp.float32

    def per_device(queries, keys, values, theta, mix, gain, out_weight, turn_lengths):
        hbm = pl.BlockSpec(memory_space=pltpu.HBM)
        vmem = pl.BlockSpec(memory_space=pltpu.VMEM)
        far = max(ring_y - 1, 1)
        return pl.pallas_call(
            functools.partial(kernel, pb_size, ha_size),
            out_shape=jax.ShapeDtypeStruct((ROWS, COLS), bf16),
            in_specs=[hbm] * 8,
            out_specs=vmem,
            scratch_shapes=[
                pltpu.SMEM(turn_lengths.shape, jnp.int32),
                pltpu.VMEM((QCONV, GROUP, KCONV), f32),
                pltpu.SMEM(mix.shape, f32),
                pltpu.VMEM((1, COLS), f32),
                pltpu.VMEM((QROWS, COLS), bf16),
                pltpu.VMEM((SPAN, COLS), bf16),
                pltpu.VMEM((SPAN, COLS), bf16),
                pltpu.VMEM(out_weight.shape, bf16),
                pltpu.VMEM((QCONV, 8, DH), f32),
                pltpu.VMEM((GROUP, QCONV * DH, DH), bf16),
                pltpu.VMEM((QROWS, DH), jnp.int32),
                pltpu.VMEM((QROWS, DH), jnp.int32),
                pltpu.VMEM((QCONV, ROWS, DH), bf16),
                pltpu.VMEM((WINDOWS, QROWS, DH), f32),
                pltpu.VMEM((WINDOWS * ROWS, QCONV * DH), bf16),
                pltpu.VMEM((GROUP, WINDOWS, ROWS, DH), f32),
                pltpu.VMEM((GROUP * ROWS, WINDOWS * DH), bf16),
                pltpu.VMEM((GROUP, ROWS, DH), f32),
                pltpu.VMEM((WINDOWS * DH, COLS), bf16),
                pltpu.VMEM((GROUP * ROWS, COLS), f32),
                pltpu.VMEM((ROWS, COLS), bf16),
                pltpu.VMEM((ring_y, ROWS, COLS), bf16),
                pltpu.VMEM((ring_y, ROWS, COLS), bf16),
                pltpu.VMEM((far, ROWS, COLS), bf16),
                pltpu.VMEM((far, ROWS, COLS), bf16),
                pltpu.VMEM((PAD, COLS), bf16),
                pltpu.SemaphoreType.DMA((8,)),
                pltpu.SemaphoreType.DMA((2,)),
                pltpu.SemaphoreType.DMA((2,)),
                pltpu.SemaphoreType.DMA((5, 4)),
                pltpu.SemaphoreType.DMA((5, 4)),
                pltpu.SemaphoreType.DMA((ring_y,)),
                pltpu.SemaphoreType.DMA((ring_y,)),
                pltpu.SemaphoreType.DMA((far,)),
                pltpu.SemaphoreType.DMA((far,)),
            ],
            compiler_params=pltpu.CompilerParams(
                collective_id=0, has_side_effects=True, vmem_limit_bytes=56 * 1024 * 1024
            ),
        )(
            turn_lengths,
            queries,
            keys,
            values,
            jnp.transpose(theta, (1, 0, 2)),
            mix,
            gain.reshape(1, COLS),
            out_weight,
        )

    return jax.shard_map(
        per_device,
        mesh=mesh,
        in_specs=(
            P("pb", "ha"),
            P("pb", "ha"),
            P("pb", "ha"),
            P("ha", None, None),
            P("ha", None),
            P("ha"),
            P("ha", None),
            P(),
        ),
        out_specs=P("pb", "ha"),
        check_vma=False,
    )
```

```python
import functools
import math

import jax
import jax.numpy as jnp
from jax import lax
from jax.experimental import pallas as pl
from jax.experimental.pallas import tpu as pltpu
from jax.sharding import PartitionSpec as P

GROUP = 4
QCONV = 6
KCONV = 11
REACH = (KCONV - 1) // 2
MAXBACK = 5
ROWS = 128
DH = 128
COLS = GROUP * DH
RING_X = 4
CORES = 2
PAD = 16
STEP = 112
WINDOWS = 7
SPAN = PAD + (MAXBACK + 1) * ROWS + PAD
QROWS = PAD + ROWS
HALF = ROWS // 2
MESH = pl.DeviceIdType.MESH
FOUR, ONE, TWO, THREE, FIVE = range(5)
FAR = 2


def slot_row(distance):
    return PAD + (MAXBACK - distance) * ROWS


def kernel(
    pb_size,
    ha_size,
    turns_hbm,
    q_hbm,
    k_hbm,
    v_hbm,
    theta_hbm,
    mix_hbm,
    gain_hbm,
    w_hbm,
    out_ref,
    turns_ref,
    theta_ref,
    mix_ref,
    gain_ref,
    qext,
    kwin,
    vwin,
    w_vmem,
    taps,
    band,
    row_lo,
    row_hi,
    row_ok,
    shifted,
    lhs,
    conv_buf,
    probs,
    inv_total,
    vext,
    acc,
    normed,
    core_out,
    core_in,
    chip_out,
    chip_in,
    q_behind,
    load_sem,
    tail_send,
    tail_recv,
    send_sem,
    recv_sem,
    core_send,
    core_recv,
    chip_send,
    chip_recv,
):
    pb = lax.axis_index("pb")
    ha = lax.axis_index("ha")
    ring_z = pb_size // RING_X
    ring_y = ha_size // CORES
    x, z = pb % RING_X, pb // RING_X
    core, y = ha % CORES, ha // CORES

    def at(new_z, new_x):
        return ((new_z % ring_z) * RING_X + new_x % RING_X, ha)

    x_next, x_over, x_back = at(z, x + 1), at(z, x + 2), at(z, x + RING_X - 1)
    z_next, z_back = at(z + 1, x), at(z + ring_z - 1, x)
    twin = (pb, y * CORES + 1 - core)

    def chip(k):
        return (pb, ((y + k) % ring_y) * CORES + core)

    own = slot_row(0)
    loads = [
        pltpu.make_async_copy(k_hbm, kwin.at[pl.ds(own, ROWS)], load_sem.at[0]),
        pltpu.make_async_copy(v_hbm, vwin.at[pl.ds(own, ROWS)], load_sem.at[1]),
        pltpu.make_async_copy(q_hbm, qext.at[pl.ds(PAD, ROWS)], load_sem.at[2]),
        pltpu.make_async_copy(turns_hbm, turns_ref, load_sem.at[4]),
        pltpu.make_async_copy(theta_hbm, theta_ref, load_sem.at[5]),
        pltpu.make_async_copy(mix_hbm, mix_ref, load_sem.at[6]),
        pltpu.make_async_copy(gain_hbm, gain_ref, load_sem.at[7]),
        pltpu.make_async_copy(w_hbm, w_vmem, load_sem.at[3]),
    ]
    for load in loads:
        load.start()

    barrier = pltpu.get_barrier_semaphore()
    has_next, has_back = z < ring_z - 1, z > 0
    greeted = [x_next, x_over, x_back, twin]
    greeted += [chip(k) for k in range(1, ring_y)]

    def greet(other):
        pl.semaphore_signal(barrier, inc=1, device_id=other, device_id_type=MESH)

    for other in greeted:
        greet(other)

    @pl.when(has_next)
    def _():
        greet(z_next)

    @pl.when(has_back)
    def _():
        greet(z_back)

    for win in (kwin, vwin):
        for distance in range(1, MAXBACK + 1):

            @pl.when(pb < distance)
            def _(win=win, row=slot_row(distance)):
                win[row : row + ROWS] = jnp.zeros((ROWS, COLS), jnp.bfloat16)

    @pl.when(pb < 1)
    def _():
        qext[0:PAD] = jnp.zeros((PAD, COLS), jnp.bfloat16)

    pl.semaphore_wait(
        barrier, len(greeted) + has_next.astype(jnp.int32) + has_back.astype(jnp.int32)
    )

    def arrived(kind, chunk):
        distance = {ONE: 1, TWO: 2, THREE: 3, FOUR: 4, FIVE: 5}[kind]

        @pl.when(pb >= distance)
        def _():
            message(kind, chunk).wait_recv()

    def message(kind, chunk):
        win = kwin if chunk < 2 else vwin
        shift = (chunk % 2) * HALF
        behind = slot_row(4)
        src, dst, target = {
            FOUR: (own, slot_row(4), z_next),
            ONE: (jnp.where(x < 3, own, behind), slot_row(1), x_next),
            TWO: (jnp.where(x < 2, own, behind), slot_row(2), x_over),
            THREE: (jnp.where(x < 1, own, behind), slot_row(3), x_back),
            FIVE: (slot_row(1), slot_row(5), z_next),
        }[kind]
        return pltpu.make_async_remote_copy(
            src_ref=win.at[pl.ds(pl.multiple_of(src + shift, 16), HALF)],
            dst_ref=win.at[pl.ds(dst + shift, HALF)],
            send_sem=send_sem.at[kind, chunk],
            recv_sem=recv_sem.at[kind, chunk],
            device_id=target,
            device_id_type=MESH,
        )

    def tail_copy(src, dst, n, target):
        return pltpu.make_async_remote_copy(
            src_ref=src,
            dst_ref=dst,
            send_sem=tail_send.at[n],
            recv_sem=tail_recv.at[n],
            device_id=target,
            device_id_type=MESH,
        )

    tail_z = tail_copy(qext.at[pl.ds(ROWS, PAD)], q_behind, 0, z_next)
    tail_own = tail_copy(qext.at[pl.ds(ROWS, PAD)], qext.at[pl.ds(0, PAD)], 1, x_next)
    tail_behind = tail_copy(q_behind, qext.at[pl.ds(0, PAD)], 1, x_next)

    def from_own(chunk):
        for kind, bound in ((ONE, 3), (TWO, 2), (THREE, 1)):

            @pl.when(x < bound)
            def _(kind=kind):
                message(kind, chunk).start()

    def from_behind(chunk):
        arrived(FOUR, chunk)
        for kind, bound in ((ONE, 3), (TWO, 2), (THREE, 1)):

            @pl.when((x >= bound) & has_back)
            def _(kind=kind):
                message(kind, chunk).start()

    def to_four(chunk):
        @pl.when(has_next)
        def _():
            message(FOUR, chunk).start()

    def to_five(chunk):
        arrived(ONE, chunk)

        @pl.when(has_next & (pb > 0))
        def _():
            message(FIVE, chunk).start()

    loads[0].wait()
    for chunk in (0, 1):
        to_four(chunk)
        from_own(chunk)
    loads[2].wait()

    @pl.when(has_next)
    def _():
        tail_z.start()

    @pl.when(x < 3)
    def _():
        tail_own.start()

    loads[1].wait()
    for chunk in (2, 3):
        to_four(chunk)
    loads[3].wait()
    loads[4].wait()
    first_row = pb * ROWS
    for win in (kwin, vwin):
        win[0:PAD] = jnp.zeros((PAD, COLS), jnp.bfloat16)
        win[SPAN - PAD : SPAN] = jnp.zeros((PAD, COLS), jnp.bfloat16)
    pos = first_row - PAD + lax.broadcasted_iota(jnp.int32, (QROWS, DH), 0)
    row_start = jnp.zeros((QROWS, DH), jnp.int32)
    start = jnp.int32(0)
    for n in range(turns_ref.shape[0]):
        row_start = jnp.where(pos >= start, start, row_start)
        start = start + turns_ref[n]
    key_zero = first_row - slot_row(0)
    row_lo[...] = row_start - key_zero
    row_hi[...] = pos - key_zero
    rel = (pos - row_start)[PAD:]
    for a in range(QCONV):
        row_ok[a] = jnp.where(rel >= a, 1.0, 0.0).astype(jnp.bfloat16)
    taps[...] = jnp.zeros(taps.shape, jnp.float32)
    scaled_theta = theta_ref[...] * (1.0 / math.sqrt(DH))
    taps[:, 0:GROUP, 0 : REACH + 1] = scaled_theta[:, :, REACH:]
    taps[:, 0:GROUP, DH - REACH : DH] = scaled_theta[:, :, :REACH]

    for chunk in (0, 1):
        from_behind(chunk)

    @pl.when(has_back)
    def _():
        tail_z.wait_recv()

    @pl.when((x == 3) & has_back)
    def _():
        tail_behind.start()

    for chunk in (2, 3):
        from_own(chunk)

    def make_band(h, carry):
        for a in range(QCONV):
            line = jnp.broadcast_to(taps[a, pl.ds(h, 1), :], (DH, DH))
            square = pltpu.roll(line, 0, 1, stride=1, stride_axis=0)
            band[h, a * DH : (a + 1) * DH, :] = square.astype(jnp.bfloat16)
        return carry

    lax.fori_loop(0, GROUP, make_band, 0)
    to_five(0)
    to_five(1)
    from_behind(2)
    from_behind(3)

    @pl.when(pb >= 1)
    def _():
        tail_own.wait_recv()

    for chunk in (0, 1):
        arrived(TWO, chunk)
        arrived(THREE, chunk)

    lane = lax.broadcasted_iota(jnp.int32, (ROWS, DH), 1)
    q_lane = lax.broadcasted_iota(jnp.int32, (QROWS, DH), 1)
    inner = (lane >= 8) & (lane < 8 + STEP)

    def convolve(h, windows):
        cols = pl.ds(pl.multiple_of(h * DH, DH), DH)
        q_head = qext[:, cols]
        for t in windows:
            k_head = kwin[t * STEP : t * STEP + DH, cols]
            scores = lax.dot_general(
                q_head, k_head, (((1,), (1,)), ((), ())), preferred_element_type=jnp.float32
            )
            place = q_lane + t * STEP
            seen = (place >= row_lo[...]) & (place <= row_hi[...])
            shifted[t] = jnp.where(seen, scores, 0.0)
        for t in windows:
            for a in range(QCONV):
                moved = shifted[t, PAD - a : PAD - a + ROWS, :].astype(jnp.bfloat16)
                lhs[t * ROWS : (t + 1) * ROWS, a * DH : (a + 1) * DH] = moved * row_ok[a]
        top, end = windows[0], windows[-1] + 1
        conv = jnp.dot(
            lhs[top * ROWS : end * ROWS], band[h], preferred_element_type=jnp.float32
        )
        lo, hi = row_lo[PAD:], row_hi[PAD:]
        for t in windows:
            place = lane + t * STEP
            kept = (place >= lo) & (place <= hi) & inner
            piece = conv[(t - top) * ROWS : (t - top + 1) * ROWS]
            conv_buf[h, t] = jnp.where(kept, piece, -1e30)

    near, far = list(range(FAR, WINDOWS)), list(range(FAR))

    def near_head(h, carry):
        convolve(h, near)
        for when, chunk in ((1, 2), (2, 3)):

            @pl.when((h == when) & (x > 0))
            def _(chunk=chunk):
                to_five(chunk)

        return carry

    lax.fori_loop(0, GROUP, near_head, 0)

    @pl.when(x == 0)
    def _():
        to_five(2)
        to_five(3)

    for chunk in (0, 1):
        arrived(FIVE, chunk)

    def far_head(h, carry):
        convolve(h, far)
        peak = conv_buf[h, 0]
        for t in range(1, WINDOWS):
            peak = jnp.maximum(peak, conv_buf[h, t])
        peak = jnp.max(peak, axis=1, keepdims=True)
        total = jnp.zeros((ROWS, DH), jnp.float32)
        rows = pl.ds(pl.multiple_of(h * ROWS, ROWS), ROWS)
        for t in range(WINDOWS):
            weights = jnp.exp(conv_buf[h, t] - peak)
            total = total + weights
            probs[rows, t * DH : (t + 1) * DH] = weights.astype(jnp.bfloat16)
        total = jnp.sum(total, axis=1, keepdims=True)
        inv_total[h] = jnp.broadcast_to(1.0 / total, (ROWS, DH))
        return carry

    lax.fori_loop(0, GROUP, far_head, 0)
    split = FAR * DH
    for chunk in (2, 3):
        arrived(TWO, chunk)
        arrived(THREE, chunk)
    for t in near:
        vext[t * DH : (t + 1) * DH] = vwin[t * STEP : t * STEP + DH]

    def near_values(p, carry):
        rows = pl.ds(pl.multiple_of(p * ROWS, ROWS), ROWS)
        acc[rows] = jnp.dot(
            probs[rows, split:], vext[split:], preferred_element_type=jnp.float32
        )
        return carry

    lax.fori_loop(0, GROUP, near_values, 0)
    for chunk in (2, 3):
        arrived(FIVE, chunk)
    for t in far:
        vext[t * DH : (t + 1) * DH] = vwin[t * STEP : t * STEP + DH]

    def far_values(p, carry):
        rows = pl.ds(pl.multiple_of(p * ROWS, ROWS), ROWS)
        acc[rows] += jnp.dot(
            probs[rows, :split], vext[:split], preferred_element_type=jnp.float32
        )
        return carry

    lax.fori_loop(0, GROUP, far_values, 0)
    for load in loads[5:]:
        load.wait()
    for h in range(GROUP):
        attn = jnp.zeros((ROWS, DH), jnp.float32)
        for p in range(GROUP):
            piece = acc[p * ROWS : (p + 1) * ROWS, h * DH : (h + 1) * DH] * inv_total[p]
            attn = attn + mix_ref[h, p] * piece
        mean_sq = jnp.mean(attn * attn, axis=1, keepdims=True)
        scaled = attn * lax.rsqrt(mean_sq + 1e-06) * gain_ref[:, h * DH : (h + 1) * DH]
        normed[:, h * DH : (h + 1) * DH] = scaled.astype(jnp.bfloat16)

    def partial(k, side):
        group = ((y + k) % ring_y) * CORES + side
        cols = pl.ds(pl.multiple_of(group * COLS, COLS), COLS)
        return jnp.dot(normed[...], w_vmem[:, cols], preferred_element_type=jnp.float32)

    def to_twin(k):
        return pltpu.make_async_remote_copy(
            src_ref=core_out.at[k],
            dst_ref=core_in.at[k],
            send_sem=core_send.at[k],
            recv_sem=core_recv.at[k],
            device_id=twin,
            device_id_type=MESH,
        )

    def to_chip(k):
        return pltpu.make_async_remote_copy(
            src_ref=chip_out.at[k - 1],
            dst_ref=chip_in.at[k - 1],
            send_sem=chip_send.at[k - 1],
            recv_sem=chip_recv.at[k - 1],
            device_id=chip(k),
            device_id_type=MESH,
        )

    order = [2, 1, 3, 0] if ring_y == 4 else list(range(ring_y - 1, -1, -1))
    for k in order:
        core_out[k] = partial(k, 1 - core).astype(jnp.bfloat16)
        to_twin(k).start()
    for k in order:
        mine = partial(k, core).astype(jnp.bfloat16).astype(jnp.float32)
        to_twin(k).wait_recv()
        both = mine + core_in[k].astype(jnp.float32)
        if k:
            chip_out[k - 1] = both.astype(jnp.bfloat16)
            to_chip(k).start()
        else:
            acc[0:ROWS] = both
    result = acc[0:ROWS]
    for k in sorted(order[:-1], key=lambda k: k == 2):
        to_chip(k).wait_recv()
        result = result + chip_in[k - 1].astype(jnp.float32)
    out_ref[...] = result.astype(jnp.bfloat16)

    sends = {
        ONE: (x < 3) | has_back,
        TWO: (x < 2) | has_back,
        THREE: (x < 1) | has_back,
        FOUR: has_next,
        FIVE: has_next & (pb > 0),
    }
    for kind, sent in sends.items():

        @pl.when(sent)
        def _(kind=kind):
            for chunk in range(4):
                message(kind, chunk).wait_send()

    @pl.when(has_next)
    def _():
        tail_z.wait_send()

    @pl.when((x < 3) | has_back)
    def _():
        tail_own.wait_send()

    for k in order:
        to_twin(k).wait_send()
        if k:
            to_chip(k).wait_send()


def solution(mesh):
    pb_size, ha_size = mesh.shape["pb"], mesh.shape["ha"]
    ring_y = ha_size // CORES
    bf16, f32 = jnp.bfloat16, jnp.float32

    def per_device(queries, keys, values, theta, mix, gain, out_weight, turn_lengths):
        hbm = pl.BlockSpec(memory_space=pltpu.HBM)
        vmem = pl.BlockSpec(memory_space=pltpu.VMEM)
        far = max(ring_y - 1, 1)
        return pl.pallas_call(
            functools.partial(kernel, pb_size, ha_size),
            out_shape=jax.ShapeDtypeStruct((ROWS, COLS), bf16),
            in_specs=[hbm] * 8,
            out_specs=vmem,
            scratch_shapes=[
                pltpu.SMEM(turn_lengths.shape, jnp.int32),
                pltpu.VMEM((QCONV, GROUP, KCONV), f32),
                pltpu.SMEM(mix.shape, f32),
                pltpu.VMEM((1, COLS), f32),
                pltpu.VMEM((QROWS, COLS), bf16),
                pltpu.VMEM((SPAN, COLS), bf16),
                pltpu.VMEM((SPAN, COLS), bf16),
                pltpu.VMEM(out_weight.shape, bf16),
                pltpu.VMEM((QCONV, 8, DH), f32),
                pltpu.VMEM((GROUP, QCONV * DH, DH), bf16),
                pltpu.VMEM((QROWS, DH), jnp.int32),
                pltpu.VMEM((QROWS, DH), jnp.int32),
                pltpu.VMEM((QCONV, ROWS, DH), bf16),
                pltpu.VMEM((WINDOWS, QROWS, DH), f32),
                pltpu.VMEM((WINDOWS * ROWS, QCONV * DH), bf16),
                pltpu.VMEM((GROUP, WINDOWS, ROWS, DH), f32),
                pltpu.VMEM((GROUP * ROWS, WINDOWS * DH), bf16),
                pltpu.VMEM((GROUP, ROWS, DH), f32),
                pltpu.VMEM((WINDOWS * DH, COLS), bf16),
                pltpu.VMEM((GROUP * ROWS, COLS), f32),
                pltpu.VMEM((ROWS, COLS), bf16),
                pltpu.VMEM((ring_y, ROWS, COLS), bf16),
                pltpu.VMEM((ring_y, ROWS, COLS), bf16),
                pltpu.VMEM((far, ROWS, COLS), bf16),
                pltpu.VMEM((far, ROWS, COLS), bf16),
                pltpu.VMEM((PAD, COLS), bf16),
                pltpu.SemaphoreType.DMA((8,)),
                pltpu.SemaphoreType.DMA((2,)),
                pltpu.SemaphoreType.DMA((2,)),
                pltpu.SemaphoreType.DMA((5, 4)),
                pltpu.SemaphoreType.DMA((5, 4)),
                pltpu.SemaphoreType.DMA((ring_y,)),
                pltpu.SemaphoreType.DMA((ring_y,)),
                pltpu.SemaphoreType.DMA((far,)),
                pltpu.SemaphoreType.DMA((far,)),
            ],
            compiler_params=pltpu.CompilerParams(
                collective_id=0, has_side_effects=True, vmem_limit_bytes=56 * 1024 * 1024
            ),
        )(
            turn_lengths,
            queries,
            keys,
            values,
            jnp.transpose(theta, (1, 0, 2)),
            mix,
            gain.reshape(1, COLS),
            out_weight,
        )

    return jax.shard_map(
        per_device,
        mesh=mesh,
        in_specs=(
            P("pb", "ha"),
            P("pb", "ha"),
            P("pb", "ha"),
            P("ha", None, None),
            P("ha", None),
            P("ha"),
            P("ha", None),
            P(),
        ),
        out_specs=P("pb", "ha"),
        check_vma=False,
    )
```

```python
import functools
import math

import jax
import jax.numpy as jnp
from jax import lax
from jax.experimental import pallas as pl
from jax.experimental.pallas import tpu as pltpu
from jax.sharding import PartitionSpec as P

GROUP = 4
QCONV = 6
KCONV = 11
REACH = (KCONV - 1) // 2
MAXBACK = 5
ROWS = 128
DH = 128
COLS = GROUP * DH
RING_X = 4
CORES = 2
PAD = 16
STEP = 112
WINDOWS = 7
SPAN = PAD + (MAXBACK + 1) * ROWS + PAD
QROWS = PAD + ROWS
MESH = pl.DeviceIdType.MESH
FOUR, ONE, TWO, THREE, FIVE, TWO_BACK = range(6)
PHASES = ((6, 5, 2), (4, 3), (0, 1))
FAR = 2
CHUNKS = 4
CHUNK = ROWS // CHUNKS
KEY_CHUNKS = tuple(range(CHUNKS))
VALUE_CHUNKS = tuple(range(CHUNKS, 2 * CHUNKS))


def slot_row(distance):
    return PAD + (MAXBACK - distance) * ROWS


def kernel(
    pb_size,
    ha_size,
    turns_hbm,
    q_hbm,
    k_hbm,
    v_hbm,
    theta_hbm,
    mix_hbm,
    gain_hbm,
    w_hbm,
    out_ref,
    turns_ref,
    theta_ref,
    mix_ref,
    gain_ref,
    qext,
    kwin,
    vwin,
    w_vmem,
    taps,
    band,
    row_lo,
    row_hi,
    row_ok,
    shifted,
    lhs,
    conv_buf,
    probs,
    inv_total,
    vext,
    acc,
    normed,
    core_out,
    core_in,
    chip_out,
    chip_in,
    q_behind,
    load_sem,
    tail_send,
    tail_recv,
    send_sem,
    recv_sem,
    core_send,
    core_recv,
    chip_send,
    chip_recv,
):
    pb = lax.axis_index("pb")
    ha = lax.axis_index("ha")
    ring_z = pb_size // RING_X
    ring_y = ha_size // CORES
    x, z = pb % RING_X, pb // RING_X
    core, y = ha % CORES, ha // CORES

    def at(new_z, new_x):
        return ((new_z % ring_z) * RING_X + new_x % RING_X, ha)

    x_next, x_over, x_back = at(z, x + 1), at(z, x + 2), at(z, x + RING_X - 1)
    z_next, z_back = at(z + 1, x), at(z + ring_z - 1, x)
    twin = (pb, y * CORES + 1 - core)

    def chip(k):
        return (pb, ((y + k) % ring_y) * CORES + core)

    own = slot_row(0)
    loads = [
        pltpu.make_async_copy(k_hbm, kwin.at[pl.ds(own, ROWS)], load_sem.at[0]),
        pltpu.make_async_copy(v_hbm, vwin.at[pl.ds(own, ROWS)], load_sem.at[1]),
        pltpu.make_async_copy(q_hbm, qext.at[pl.ds(PAD, ROWS)], load_sem.at[2]),
        pltpu.make_async_copy(turns_hbm, turns_ref, load_sem.at[4]),
        pltpu.make_async_copy(theta_hbm, theta_ref, load_sem.at[5]),
        pltpu.make_async_copy(mix_hbm, mix_ref, load_sem.at[6]),
        pltpu.make_async_copy(gain_hbm, gain_ref, load_sem.at[7]),
        pltpu.make_async_copy(w_hbm, w_vmem, load_sem.at[3]),
    ]
    for load in loads:
        load.start()

    barrier = pltpu.get_barrier_semaphore()
    has_next, has_back = z < ring_z - 1, z > 0
    greeted = [x_next, x_over, x_back, twin]
    greeted += [chip(k) for k in range(1, ring_y)]

    def greet(other):
        pl.semaphore_signal(barrier, inc=1, device_id=other, device_id_type=MESH)

    for other in greeted:
        greet(other)

    @pl.when(has_next)
    def _():
        greet(z_next)

    @pl.when(has_back)
    def _():
        greet(z_back)

    for win in (kwin, vwin):
        for distance in range(1, MAXBACK + 1):

            @pl.when(pb < distance)
            def _(win=win, row=slot_row(distance)):
                win[row : row + ROWS] = jnp.zeros((ROWS, COLS), jnp.bfloat16)

    @pl.when(pb < 1)
    def _():
        qext[0:PAD] = jnp.zeros((PAD, COLS), jnp.bfloat16)

    pl.semaphore_wait(
        barrier, len(greeted) + has_next.astype(jnp.int32) + has_back.astype(jnp.int32)
    )

    def arrived(kind, chunk):
        distance = {ONE: 1, TWO: 2, THREE: 3, FOUR: 4, FIVE: 5}[kind]

        @pl.when(pb >= distance)
        def _():
            message(kind, chunk).wait_recv()

    def message(kind, chunk):
        win = kwin if chunk < CHUNKS else vwin
        shift = (chunk % CHUNKS) * CHUNK
        behind = slot_row(4)
        src, dst, target = {
            FOUR: (own, slot_row(4), z_next),
            ONE: (jnp.where(x < 3, own, behind), slot_row(1), x_next),
            TWO: (jnp.where(x < 2, own, behind), slot_row(2), x_over),
            THREE: (jnp.where(x < 1, own, behind), slot_row(3), x_back),
            FIVE: (slot_row(1), slot_row(5), z_next),
            TWO_BACK: (slot_row(3), slot_row(2), x_back),
        }[kind]
        if kind == TWO and chunk >= CHUNKS:
            src, dst, target = slot_row(1), slot_row(2), x_next
        return pltpu.make_async_remote_copy(
            src_ref=win.at[pl.ds(pl.multiple_of(src + shift, 16), CHUNK)],
            dst_ref=win.at[pl.ds(dst + shift, CHUNK)],
            send_sem=send_sem.at[kind, chunk],
            recv_sem=recv_sem.at[TWO if kind == TWO_BACK else kind, chunk],
            device_id=target,
            device_id_type=MESH,
        )

    def tail_copy(src, dst, n, target):
        return pltpu.make_async_remote_copy(
            src_ref=src,
            dst_ref=dst,
            send_sem=tail_send.at[n],
            recv_sem=tail_recv.at[n],
            device_id=target,
            device_id_type=MESH,
        )

    tail_z = tail_copy(qext.at[pl.ds(ROWS, PAD)], q_behind, 0, z_next)
    tail_own = tail_copy(qext.at[pl.ds(ROWS, PAD)], qext.at[pl.ds(0, PAD)], 1, x_next)
    tail_behind = tail_copy(q_behind, qext.at[pl.ds(0, PAD)], 1, x_next)

    def steps(chunk):
        two = ((TWO, 2),) if chunk < CHUNKS else ()
        return ((ONE, 3), *two, (THREE, 1))

    def from_own(chunk):
        for kind, bound in steps(chunk):

            @pl.when(x < bound)
            def _(kind=kind):
                message(kind, chunk).start()

    def from_behind(chunk):
        arrived(FOUR, chunk)
        for kind, bound in steps(chunk):

            @pl.when((x >= bound) & has_back)
            def _(kind=kind):
                message(kind, chunk).start()

    def to_four(chunk):
        @pl.when(has_next)
        def _():
            message(FOUR, chunk).start()

    def to_five(chunk):
        arrived(ONE, chunk)

        @pl.when(has_next & (pb > 0))
        def _():
            message(FIVE, chunk).start()

    def to_two(chunk):
        @pl.when((x < 3) & (pb > 0))
        def _():
            message(TWO, chunk).start()

    def back_to_two(chunk):
        @pl.when((x == 1) & has_back)
        def _():
            message(THREE, chunk).wait_recv()
            message(TWO_BACK, chunk).start()

    loads[0].wait()
    for chunk in KEY_CHUNKS:
        to_four(chunk)
        from_own(chunk)
    loads[2].wait()

    @pl.when(has_next)
    def _():
        tail_z.start()

    @pl.when(x < 3)
    def _():
        tail_own.start()

    loads[1].wait()
    for chunk in VALUE_CHUNKS:
        to_four(chunk)
    loads[3].wait()
    loads[4].wait()
    first_row = pb * ROWS
    for win in (kwin, vwin):
        win[0:PAD] = jnp.zeros((PAD, COLS), jnp.bfloat16)
        win[SPAN - PAD : SPAN] = jnp.zeros((PAD, COLS), jnp.bfloat16)
    pos = first_row - PAD + lax.broadcasted_iota(jnp.int32, (QROWS, DH), 0)
    row_start = jnp.zeros((QROWS, DH), jnp.int32)
    start = jnp.int32(0)
    for n in range(turns_ref.shape[0]):
        row_start = jnp.where(pos >= start, start, row_start)
        start = start + turns_ref[n]
    key_zero = first_row - slot_row(0)
    row_lo[...] = row_start - key_zero
    row_hi[...] = pos - key_zero
    rel = (pos - row_start)[PAD:]
    for a in range(QCONV):
        row_ok[a] = jnp.where(rel >= a, 1.0, 0.0).astype(jnp.bfloat16)
    taps[...] = jnp.zeros(taps.shape, jnp.float32)
    scaled_theta = theta_ref[...] * (1.0 / math.sqrt(DH))
    taps[:, 0:GROUP, 0 : REACH + 1] = scaled_theta[:, :, REACH:]
    taps[:, 0:GROUP, DH - REACH : DH] = scaled_theta[:, :, :REACH]

    for chunk in KEY_CHUNKS:
        from_behind(chunk)

    @pl.when(has_back)
    def _():
        tail_z.wait_recv()

    @pl.when((x == 3) & has_back)
    def _():
        tail_behind.start()

    for chunk in VALUE_CHUNKS:
        from_own(chunk)

    def make_band(h, carry):
        for a in range(QCONV):
            line = jnp.broadcast_to(taps[a, pl.ds(h, 1), :], (DH, DH))
            square = pltpu.roll(line, 0, 1, stride=1, stride_axis=0)
            band[h, a * DH : (a + 1) * DH, :] = square.astype(jnp.bfloat16)
        return carry

    lax.fori_loop(0, GROUP, make_band, 0)
    for chunk in KEY_CHUNKS:
        to_five(chunk)

    @pl.when(pb >= 1)
    def _():
        tail_own.wait_recv()

    lane = lax.broadcasted_iota(jnp.int32, (ROWS, DH), 1)
    q_lane = lax.broadcasted_iota(jnp.int32, (QROWS, DH), 1)
    inner = (lane >= 8) & (lane < 8 + STEP)

    def convolve(windows):
        for h in range(GROUP):
            q_head = qext[:, h * DH : (h + 1) * DH]
            for t in windows:
                k_head = kwin[t * STEP : t * STEP + DH, h * DH : (h + 1) * DH]
                scores = lax.dot_general(
                    q_head,
                    k_head,
                    (((1,), (1,)), ((), ())),
                    preferred_element_type=jnp.float32,
                )
                place = q_lane + t * STEP
                seen = (place >= row_lo[...]) & (place <= row_hi[...])
                shifted[h, t] = jnp.where(seen, scores, 0.0)
        for h in range(GROUP):
            for n, t in enumerate(windows):
                for a in range(QCONV):
                    moved = shifted[h, t, PAD - a : PAD - a + ROWS, :].astype(jnp.bfloat16)
                    lhs[h, n * ROWS : (n + 1) * ROWS, a * DH : (a + 1) * DH] = (
                        moved * row_ok[a]
                    )
        lo, hi = row_lo[PAD:], row_hi[PAD:]
        for h in range(GROUP):
            conv = jnp.dot(
                lhs[h, : len(windows) * ROWS], band[h], preferred_element_type=jnp.float32
            )
            for n, t in enumerate(windows):
                place = lane + t * STEP
                kept = (place >= lo) & (place <= hi) & inner
                piece = conv[n * ROWS : (n + 1) * ROWS]
                conv_buf[h, t] = jnp.where(kept, piece, -1e30)

    near, far = range(FAR, WINDOWS), range(FAR)

    for chunk in VALUE_CHUNKS:
        from_behind(chunk)
    for chunk in KEY_CHUNKS:
        arrived(THREE, chunk)
    convolve(PHASES[0])
    for chunk in VALUE_CHUNKS:
        to_five(chunk)
        to_two(chunk)
    for chunk in VALUE_CHUNKS:
        back_to_two(chunk)
    for chunk in KEY_CHUNKS:
        arrived(TWO, chunk)
    convolve(PHASES[1])
    for chunk in KEY_CHUNKS:
        arrived(FIVE, chunk)

    convolve(PHASES[2])
    for h in range(GROUP):
        peak = conv_buf[h, 0]
        for t in range(1, WINDOWS):
            peak = jnp.maximum(peak, conv_buf[h, t])
        peak = jnp.max(peak, axis=1, keepdims=True)
        total = jnp.zeros((ROWS, DH), jnp.float32)
        for t in range(WINDOWS):
            weights = jnp.exp(conv_buf[h, t] - peak)
            total = total + weights
            probs[h * ROWS : (h + 1) * ROWS, t * DH : (t + 1) * DH] = weights.astype(
                jnp.bfloat16
            )
        total = jnp.sum(total, axis=1, keepdims=True)
        inv_total[h] = jnp.broadcast_to(1.0 / total, (ROWS, DH))
    split = FAR * DH
    for chunk in VALUE_CHUNKS:
        arrived(TWO, chunk)

        @pl.when((pb >= 3) & (x != 1))
        def _(chunk=chunk):
            message(THREE, chunk).wait_recv()

    for t in near:
        vext[t * DH : (t + 1) * DH] = vwin[t * STEP : t * STEP + DH]

    acc[...] = jnp.dot(probs[:, split:], vext[split:], preferred_element_type=jnp.float32)
    for chunk in VALUE_CHUNKS:
        arrived(FIVE, chunk)
    for t in far:
        vext[t * DH : (t + 1) * DH] = vwin[t * STEP : t * STEP + DH]

    acc[...] += jnp.dot(probs[:, :split], vext[:split], preferred_element_type=jnp.float32)
    for load in loads[5:]:
        load.wait()
    for h in range(GROUP):
        attn = jnp.zeros((ROWS, DH), jnp.float32)
        for p in range(GROUP):
            piece = acc[p * ROWS : (p + 1) * ROWS, h * DH : (h + 1) * DH] * inv_total[p]
            attn = attn + mix_ref[h, p] * piece
        mean_sq = jnp.mean(attn * attn, axis=1, keepdims=True)
        scaled = attn * lax.rsqrt(mean_sq + 1e-06) * gain_ref[:, h * DH : (h + 1) * DH]
        normed[:, h * DH : (h + 1) * DH] = scaled.astype(jnp.bfloat16)

    def partial(k, side):
        group = ((y + k) % ring_y) * CORES + side
        cols = pl.ds(pl.multiple_of(group * COLS, COLS), COLS)
        return jnp.dot(normed[...], w_vmem[:, cols], preferred_element_type=jnp.float32)

    def to_twin(k):
        return pltpu.make_async_remote_copy(
            src_ref=core_out.at[k],
            dst_ref=core_in.at[k],
            send_sem=core_send.at[k],
            recv_sem=core_recv.at[k],
            device_id=twin,
            device_id_type=MESH,
        )

    def to_chip(k):
        return pltpu.make_async_remote_copy(
            src_ref=chip_out.at[k - 1],
            dst_ref=chip_in.at[k - 1],
            send_sem=chip_send.at[k - 1],
            recv_sem=chip_recv.at[k - 1],
            device_id=chip(k),
            device_id_type=MESH,
        )

    order = [2, 1, 3, 0] if ring_y == 4 else list(range(ring_y - 1, -1, -1))
    for k in order:
        core_out[k] = partial(k, 1 - core).astype(jnp.bfloat16)
        to_twin(k).start()
    for k in order:
        mine = partial(k, core).astype(jnp.bfloat16).astype(jnp.float32)
        to_twin(k).wait_recv()
        pair = mine + core_in[k].astype(jnp.float32)
        if k:
            chip_out[k - 1] = pair.astype(jnp.bfloat16)
            to_chip(k).start()
        else:
            acc[0:ROWS] = pair
    result = acc[0:ROWS]
    for k in sorted(order[:-1], key=lambda k: k == 2):
        to_chip(k).wait_recv()
        result = result + chip_in[k - 1].astype(jnp.float32)
    out_ref[...] = result.astype(jnp.bfloat16)

    both = KEY_CHUNKS + VALUE_CHUNKS
    sends = (
        (ONE, (x < 3) | has_back, both),
        (TWO, (x < 2) | has_back, KEY_CHUNKS),
        (TWO, (x < 3) & (pb > 0), VALUE_CHUNKS),
        (TWO_BACK, (x == 1) & has_back, VALUE_CHUNKS),
        (THREE, (x < 1) | has_back, both),
        (FOUR, has_next, both),
        (FIVE, has_next & (pb > 0), both),
    )
    for kind, sent, chunks in sends:

        @pl.when(sent)
        def _(kind=kind, chunks=chunks):
            for chunk in chunks:
                message(kind, chunk).wait_send()

    @pl.when(has_next)
    def _():
        tail_z.wait_send()

    @pl.when((x < 3) | has_back)
    def _():
        tail_own.wait_send()

    for k in order:
        to_twin(k).wait_send()
        if k:
            to_chip(k).wait_send()


def solution(mesh):
    pb_size, ha_size = mesh.shape["pb"], mesh.shape["ha"]
    ring_y = ha_size // CORES
    bf16, f32 = jnp.bfloat16, jnp.float32

    def per_device(queries, keys, values, theta, mix, gain, out_weight, turn_lengths):
        hbm = pl.BlockSpec(memory_space=pltpu.HBM)
        vmem = pl.BlockSpec(memory_space=pltpu.VMEM)
        far = max(ring_y - 1, 1)
        return pl.pallas_call(
            functools.partial(kernel, pb_size, ha_size),
            out_shape=jax.ShapeDtypeStruct((ROWS, COLS), bf16),
            in_specs=[hbm] * 8,
            out_specs=vmem,
            scratch_shapes=[
                pltpu.SMEM(turn_lengths.shape, jnp.int32),
                pltpu.VMEM((QCONV, GROUP, KCONV), f32),
                pltpu.SMEM(mix.shape, f32),
                pltpu.VMEM((1, COLS), f32),
                pltpu.VMEM((QROWS, COLS), bf16),
                pltpu.VMEM((SPAN, COLS), bf16),
                pltpu.VMEM((SPAN, COLS), bf16),
                pltpu.VMEM(out_weight.shape, bf16),
                pltpu.VMEM((QCONV, 8, DH), f32),
                pltpu.VMEM((GROUP, QCONV * DH, DH), bf16),
                pltpu.VMEM((QROWS, DH), jnp.int32),
                pltpu.VMEM((QROWS, DH), jnp.int32),
                pltpu.VMEM((QCONV, ROWS, DH), bf16),
                pltpu.VMEM((GROUP, WINDOWS, QROWS, DH), f32),
                pltpu.VMEM((GROUP, WINDOWS * ROWS, QCONV * DH), bf16),
                pltpu.VMEM((GROUP, WINDOWS, ROWS, DH), f32),
                pltpu.VMEM((GROUP * ROWS, WINDOWS * DH), bf16),
                pltpu.VMEM((GROUP, ROWS, DH), f32),
                pltpu.VMEM((WINDOWS * DH, COLS), bf16),
                pltpu.VMEM((GROUP * ROWS, COLS), f32),
                pltpu.VMEM((ROWS, COLS), bf16),
                pltpu.VMEM((ring_y, ROWS, COLS), bf16),
                pltpu.VMEM((ring_y, ROWS, COLS), bf16),
                pltpu.VMEM((far, ROWS, COLS), bf16),
                pltpu.VMEM((far, ROWS, COLS), bf16),
                pltpu.VMEM((PAD, COLS), bf16),
                pltpu.SemaphoreType.DMA((8,)),
                pltpu.SemaphoreType.DMA((2,)),
                pltpu.SemaphoreType.DMA((2,)),
                pltpu.SemaphoreType.DMA((6, 2 * CHUNKS)),
                pltpu.SemaphoreType.DMA((6, 2 * CHUNKS)),
                pltpu.SemaphoreType.DMA((ring_y,)),
                pltpu.SemaphoreType.DMA((ring_y,)),
                pltpu.SemaphoreType.DMA((far,)),
                pltpu.SemaphoreType.DMA((far,)),
            ],
            compiler_params=pltpu.CompilerParams(
                collective_id=0, has_side_effects=True, vmem_limit_bytes=56 * 1024 * 1024
            ),
        )(
            turn_lengths,
            queries,
            keys,
            values,
            jnp.transpose(theta, (1, 0, 2)),
            mix,
            gain.reshape(1, COLS),
            out_weight,
        )

    return jax.shard_map(
        per_device,
        mesh=mesh,
        in_specs=(
            P("pb", "ha"),
            P("pb", "ha"),
            P("pb", "ha"),
            P("ha", None, None),
            P("ha", None),
            P("ha"),
            P("ha", None),
            P(),
        ),
        out_specs=P("pb", "ha"),
        check_vma=False,
    )
```

```python
import functools
import math

import jax
import jax.numpy as jnp
from jax import lax
from jax.experimental import pallas as pl
from jax.experimental.pallas import tpu as pltpu
from jax.sharding import PartitionSpec as P

GROUP = 4
QCONV = 6
KCONV = 11
REACH = (KCONV - 1) // 2
MAXBACK = 5
ROWS = 128
DH = 128
COLS = GROUP * DH
RING_X = 4
CORES = 2
PAD = 16
STEP = 112
WINDOWS = 7
SPAN = PAD + (MAXBACK + 1) * ROWS + PAD
QROWS = PAD + ROWS
MESH = pl.DeviceIdType.MESH
FOUR, ONE, TWO, THREE, FIVE, TWO_BACK = range(6)
PHASES = ((6, 5, 2), (4, 3), (0, 1))
FAR = 2
CHUNKS = 4
CHUNK = ROWS // CHUNKS
KEY_CHUNKS = tuple(range(CHUNKS))
VALUE_CHUNKS = tuple(range(CHUNKS, 2 * CHUNKS))


def slot_row(distance):
    return PAD + (MAXBACK - distance) * ROWS


def kernel(
    pb_size,
    ha_size,
    turns_hbm,
    q_hbm,
    k_hbm,
    v_hbm,
    theta_hbm,
    mix_hbm,
    gain_hbm,
    w_hbm,
    out_ref,
    turns_ref,
    theta_ref,
    mix_ref,
    gain_ref,
    qext,
    kwin,
    vwin,
    w_vmem,
    taps,
    band,
    row_lo,
    row_hi,
    row_ok,
    shifted,
    lhs,
    conv_buf,
    probs,
    inv_total,
    vext,
    acc,
    normed,
    core_out,
    core_in,
    chip_out,
    chip_in,
    q_behind,
    load_sem,
    tail_send,
    tail_recv,
    send_sem,
    recv_sem,
    core_send,
    core_recv,
    chip_send,
    chip_recv,
):
    pb = lax.axis_index("pb")
    ha = lax.axis_index("ha")
    ring_z = pb_size // RING_X
    ring_y = ha_size // CORES
    x, z = pb % RING_X, pb // RING_X
    core, y = ha % CORES, ha // CORES

    def at(new_z, new_x):
        return ((new_z % ring_z) * RING_X + new_x % RING_X, ha)

    x_next, x_back = at(z, x + 1), at(z, x + RING_X - 1)
    z_next, z_back = at(z + 1, x), at(z + ring_z - 1, x)
    twin = (pb, y * CORES + 1 - core)

    def chip(k):
        return (pb, ((y + k) % ring_y) * CORES + core)

    own = slot_row(0)
    loads = [
        pltpu.make_async_copy(k_hbm, kwin.at[pl.ds(own, ROWS)], load_sem.at[0]),
        pltpu.make_async_copy(v_hbm, vwin.at[pl.ds(own, ROWS)], load_sem.at[1]),
        pltpu.make_async_copy(q_hbm, qext.at[pl.ds(PAD, ROWS)], load_sem.at[2]),
        pltpu.make_async_copy(turns_hbm, turns_ref, load_sem.at[4]),
        pltpu.make_async_copy(theta_hbm, theta_ref, load_sem.at[5]),
        pltpu.make_async_copy(mix_hbm, mix_ref, load_sem.at[6]),
        pltpu.make_async_copy(gain_hbm, gain_ref, load_sem.at[7]),
        pltpu.make_async_copy(w_hbm, w_vmem, load_sem.at[3]),
    ]
    for load in loads:
        load.start()

    barrier = pltpu.get_barrier_semaphore()
    has_next, has_back = z < ring_z - 1, z > 0
    greeted = [x_next, x_back, twin]
    greeted += [chip(k) for k in range(1, ring_y)]

    def greet(other):
        pl.semaphore_signal(barrier, inc=1, device_id=other, device_id_type=MESH)

    for other in greeted:
        greet(other)

    @pl.when(has_next)
    def _():
        greet(z_next)

    @pl.when(has_back)
    def _():
        greet(z_back)

    for win in (kwin, vwin):
        for distance in range(1, MAXBACK + 1):

            @pl.when(pb < distance)
            def _(win=win, row=slot_row(distance)):
                win[row : row + ROWS] = jnp.zeros((ROWS, COLS), jnp.bfloat16)

    @pl.when(pb < 1)
    def _():
        qext[0:PAD] = jnp.zeros((PAD, COLS), jnp.bfloat16)

    pl.semaphore_wait(
        barrier, len(greeted) + has_next.astype(jnp.int32) + has_back.astype(jnp.int32)
    )

    def arrived(kind, chunk):
        distance = {ONE: 1, TWO: 2, THREE: 3, FOUR: 4, FIVE: 5}[kind]

        @pl.when(pb >= distance)
        def _():
            message(kind, chunk).wait_recv()

    def message(kind, chunk):
        win = kwin if chunk < CHUNKS else vwin
        shift = (chunk % CHUNKS) * CHUNK
        behind = slot_row(4)
        src, dst, target = {
            FOUR: (own, slot_row(4), z_next),
            ONE: (jnp.where(x < 3, own, behind), slot_row(1), x_next),
            TWO: (slot_row(1), slot_row(2), x_next),
            THREE: (jnp.where(x < 1, own, behind), slot_row(3), x_back),
            FIVE: (slot_row(1), slot_row(5), z_next),
            TWO_BACK: (slot_row(3), slot_row(2), x_back),
        }[kind]
        return pltpu.make_async_remote_copy(
            src_ref=win.at[pl.ds(pl.multiple_of(src + shift, 16), CHUNK)],
            dst_ref=win.at[pl.ds(dst + shift, CHUNK)],
            send_sem=send_sem.at[kind, chunk],
            recv_sem=recv_sem.at[TWO if kind == TWO_BACK else kind, chunk],
            device_id=target,
            device_id_type=MESH,
        )

    def tail_copy(src, dst, n, target):
        return pltpu.make_async_remote_copy(
            src_ref=src,
            dst_ref=dst,
            send_sem=tail_send.at[n],
            recv_sem=tail_recv.at[n],
            device_id=target,
            device_id_type=MESH,
        )

    tail_z = tail_copy(qext.at[pl.ds(ROWS, PAD)], q_behind, 0, z_next)
    tail_own = tail_copy(qext.at[pl.ds(ROWS, PAD)], qext.at[pl.ds(0, PAD)], 1, x_next)
    tail_behind = tail_copy(q_behind, qext.at[pl.ds(0, PAD)], 1, x_next)

    def steps(chunk):
        return ((ONE, 3), (THREE, 1))

    def from_own(chunk):
        for kind, bound in steps(chunk):

            @pl.when(x < bound)
            def _(kind=kind):
                message(kind, chunk).start()

    def from_behind(chunk):
        arrived(FOUR, chunk)
        for kind, bound in steps(chunk):

            @pl.when((x >= bound) & has_back)
            def _(kind=kind):
                message(kind, chunk).start()

    def to_four(chunk):
        @pl.when(has_next)
        def _():
            message(FOUR, chunk).start()

    def to_five(chunk):
        arrived(ONE, chunk)

        @pl.when(has_next & (pb > 0))
        def _():
            message(FIVE, chunk).start()

    def to_two(chunk):
        @pl.when((x < 3) & (pb > 0))
        def _():
            message(TWO, chunk).start()

    def back_to_two(chunk):
        @pl.when((x == 1) & has_back)
        def _():
            message(THREE, chunk).wait_recv()
            message(TWO_BACK, chunk).start()

    loads[2].wait()

    @pl.when(has_next)
    def _():
        tail_z.start()

    @pl.when(x < 3)
    def _():
        tail_own.start()

    loads[0].wait()
    for chunk in KEY_CHUNKS:
        to_four(chunk)
        from_own(chunk)
    loads[1].wait()
    for chunk in VALUE_CHUNKS:
        to_four(chunk)
    loads[3].wait()
    loads[4].wait()
    first_row = pb * ROWS
    for win in (kwin, vwin):
        win[0:PAD] = jnp.zeros((PAD, COLS), jnp.bfloat16)
        win[SPAN - PAD : SPAN] = jnp.zeros((PAD, COLS), jnp.bfloat16)
    pos = first_row - PAD + lax.broadcasted_iota(jnp.int32, (QROWS, DH), 0)
    row_start = jnp.zeros((QROWS, DH), jnp.int32)
    start = jnp.int32(0)
    for n in range(turns_ref.shape[0]):
        row_start = jnp.where(pos >= start, start, row_start)
        start = start + turns_ref[n]
    key_zero = first_row - slot_row(0)
    row_lo[...] = row_start - key_zero
    row_hi[...] = pos - key_zero
    rel = (pos - row_start)[PAD:]
    for a in range(QCONV):
        row_ok[a] = jnp.where(rel >= a, 1.0, 0.0).astype(jnp.bfloat16)
    taps[...] = jnp.zeros(taps.shape, jnp.float32)
    scaled_theta = theta_ref[...] * (1.0 / math.sqrt(DH))
    taps[:, 0:GROUP, 0 : REACH + 1] = scaled_theta[:, :, REACH:]
    taps[:, 0:GROUP, DH - REACH : DH] = scaled_theta[:, :, :REACH]

    @pl.when(has_back)
    def _():
        tail_z.wait_recv()

    @pl.when((x == 3) & has_back)
    def _():
        tail_behind.start()

    for chunk in KEY_CHUNKS:
        from_behind(chunk)


    for chunk in VALUE_CHUNKS:
        from_own(chunk)

    def make_band(h, carry):
        for a in range(QCONV):
            line = jnp.broadcast_to(taps[a, pl.ds(h, 1), :], (DH, DH))
            square = pltpu.roll(line, 0, 1, stride=1, stride_axis=0)
            band[h, a * DH : (a + 1) * DH, :] = square.astype(jnp.bfloat16)
        return carry

    lax.fori_loop(0, GROUP, make_band, 0)
    for chunk in KEY_CHUNKS:
        to_five(chunk)
        to_two(chunk)
    for chunk in KEY_CHUNKS:
        back_to_two(chunk)

    @pl.when(pb >= 1)
    def _():
        tail_own.wait_recv()

    lane = lax.broadcasted_iota(jnp.int32, (ROWS, DH), 1)
    q_lane = lax.broadcasted_iota(jnp.int32, (QROWS, DH), 1)
    inner = (lane >= 8) & (lane < 8 + STEP)

    def convolve(windows):
        for h in range(GROUP):
            q_head = qext[:, h * DH : (h + 1) * DH]
            for t in windows:
                k_head = kwin[t * STEP : t * STEP + DH, h * DH : (h + 1) * DH]
                scores = lax.dot_general(
                    q_head,
                    k_head,
                    (((1,), (1,)), ((), ())),
                    preferred_element_type=jnp.float32,
                )
                place = q_lane + t * STEP
                seen = (place >= row_lo[...]) & (place <= row_hi[...])
                shifted[h, t] = jnp.where(seen, scores, 0.0)
        for h in range(GROUP):
            for n, t in enumerate(windows):
                for a in range(QCONV):
                    moved = shifted[h, t, PAD - a : PAD - a + ROWS, :].astype(jnp.bfloat16)
                    lhs[h, n * ROWS : (n + 1) * ROWS, a * DH : (a + 1) * DH] = (
                        moved * row_ok[a]
                    )
        lo, hi = row_lo[PAD:], row_hi[PAD:]
        for h in range(GROUP):
            conv = jnp.dot(
                lhs[h, : len(windows) * ROWS], band[h], preferred_element_type=jnp.float32
            )
            for n, t in enumerate(windows):
                place = lane + t * STEP
                kept = (place >= lo) & (place <= hi) & inner
                piece = conv[n * ROWS : (n + 1) * ROWS]
                conv_buf[h, t] = jnp.where(kept, piece, -1e30)

    near, far = range(FAR, WINDOWS), range(FAR)

    for chunk in VALUE_CHUNKS:
        from_behind(chunk)
    for chunk in KEY_CHUNKS:

        @pl.when((pb >= 3) & (x != 1))
        def _(chunk=chunk):
            message(THREE, chunk).wait_recv()

    convolve(PHASES[0])
    for chunk in VALUE_CHUNKS:
        to_five(chunk)
        to_two(chunk)
    for chunk in VALUE_CHUNKS:
        back_to_two(chunk)
    for chunk in KEY_CHUNKS:
        arrived(TWO, chunk)
    convolve(PHASES[1])
    for chunk in KEY_CHUNKS:
        arrived(FIVE, chunk)

    convolve(PHASES[2])
    for h in range(GROUP):
        peak = conv_buf[h, 0]
        for t in range(1, WINDOWS):
            peak = jnp.maximum(peak, conv_buf[h, t])
        peak = jnp.max(peak, axis=1, keepdims=True)
        total = jnp.zeros((ROWS, DH), jnp.float32)
        for t in range(WINDOWS):
            weights = jnp.exp(conv_buf[h, t] - peak)
            total = total + weights
            probs[h * ROWS : (h + 1) * ROWS, t * DH : (t + 1) * DH] = weights.astype(
                jnp.bfloat16
            )
        total = jnp.sum(total, axis=1, keepdims=True)
        inv_total[h] = jnp.broadcast_to(1.0 / total, (ROWS, DH))
    split = FAR * DH
    for chunk in VALUE_CHUNKS:
        arrived(TWO, chunk)

        @pl.when((pb >= 3) & (x != 1))
        def _(chunk=chunk):
            message(THREE, chunk).wait_recv()

    for t in near:
        vext[t * DH : (t + 1) * DH] = vwin[t * STEP : t * STEP + DH]

    acc[...] = jnp.dot(probs[:, split:], vext[split:], preferred_element_type=jnp.float32)
    for chunk in VALUE_CHUNKS:
        arrived(FIVE, chunk)
    for t in far:
        vext[t * DH : (t + 1) * DH] = vwin[t * STEP : t * STEP + DH]

    acc[...] += jnp.dot(probs[:, :split], vext[:split], preferred_element_type=jnp.float32)
    for load in loads[5:]:
        load.wait()
    for h in range(GROUP):
        attn = jnp.zeros((ROWS, DH), jnp.float32)
        for p in range(GROUP):
            piece = acc[p * ROWS : (p + 1) * ROWS, h * DH : (h + 1) * DH] * inv_total[p]
            attn = attn + mix_ref[h, p] * piece
        mean_sq = jnp.mean(attn * attn, axis=1, keepdims=True)
        scaled = attn * lax.rsqrt(mean_sq + 1e-06) * gain_ref[:, h * DH : (h + 1) * DH]
        normed[:, h * DH : (h + 1) * DH] = scaled.astype(jnp.bfloat16)

    def partial(k, side):
        group = ((y + k) % ring_y) * CORES + side
        cols = pl.ds(pl.multiple_of(group * COLS, COLS), COLS)
        return jnp.dot(normed[...], w_vmem[:, cols], preferred_element_type=jnp.float32)

    def to_twin(k):
        return pltpu.make_async_remote_copy(
            src_ref=core_out.at[k],
            dst_ref=core_in.at[k],
            send_sem=core_send.at[k],
            recv_sem=core_recv.at[k],
            device_id=twin,
            device_id_type=MESH,
        )

    def to_chip(k):
        return pltpu.make_async_remote_copy(
            src_ref=chip_out.at[k - 1],
            dst_ref=chip_in.at[k - 1],
            send_sem=chip_send.at[k - 1],
            recv_sem=chip_recv.at[k - 1],
            device_id=chip(k),
            device_id_type=MESH,
        )

    order = [2, 1, 3, 0] if ring_y == 4 else list(range(ring_y - 1, -1, -1))
    for k in order:
        core_out[k] = partial(k, 1 - core).astype(jnp.bfloat16)
        to_twin(k).start()
    for k in order:
        mine = partial(k, core).astype(jnp.bfloat16).astype(jnp.float32)
        to_twin(k).wait_recv()
        pair = mine + core_in[k].astype(jnp.float32)
        if k:
            chip_out[k - 1] = pair.astype(jnp.bfloat16)
            to_chip(k).start()
        else:
            acc[0:ROWS] = pair
    result = acc[0:ROWS]
    for k in sorted(order[:-1], key=lambda k: k == 2):
        to_chip(k).wait_recv()
        result = result + chip_in[k - 1].astype(jnp.float32)
    out_ref[...] = result.astype(jnp.bfloat16)

    both = KEY_CHUNKS + VALUE_CHUNKS
    sends = (
        (ONE, (x < 3) | has_back, both),
        (TWO, (x < 3) & (pb > 0), both),
        (TWO_BACK, (x == 1) & has_back, both),
        (THREE, (x < 1) | has_back, both),
        (FOUR, has_next, both),
        (FIVE, has_next & (pb > 0), both),
    )
    for kind, sent, chunks in sends:

        @pl.when(sent)
        def _(kind=kind, chunks=chunks):
            for chunk in chunks:
                message(kind, chunk).wait_send()

    @pl.when(has_next)
    def _():
        tail_z.wait_send()

    @pl.when((x < 3) | has_back)
    def _():
        tail_own.wait_send()

    for k in order:
        to_twin(k).wait_send()
        if k:
            to_chip(k).wait_send()


def solution(mesh):
    pb_size, ha_size = mesh.shape["pb"], mesh.shape["ha"]
    ring_y = ha_size // CORES
    bf16, f32 = jnp.bfloat16, jnp.float32

    def per_device(queries, keys, values, theta, mix, gain, out_weight, turn_lengths):
        hbm = pl.BlockSpec(memory_space=pltpu.HBM)
        vmem = pl.BlockSpec(memory_space=pltpu.VMEM)
        far = max(ring_y - 1, 1)
        return pl.pallas_call(
            functools.partial(kernel, pb_size, ha_size),
            out_shape=jax.ShapeDtypeStruct((ROWS, COLS), bf16),
            in_specs=[hbm] * 8,
            out_specs=vmem,
            scratch_shapes=[
                pltpu.SMEM(turn_lengths.shape, jnp.int32),
                pltpu.VMEM((QCONV, GROUP, KCONV), f32),
                pltpu.SMEM(mix.shape, f32),
                pltpu.VMEM((1, COLS), f32),
                pltpu.VMEM((QROWS, COLS), bf16),
                pltpu.VMEM((SPAN, COLS), bf16),
                pltpu.VMEM((SPAN, COLS), bf16),
                pltpu.VMEM(out_weight.shape, bf16),
                pltpu.VMEM((QCONV, 8, DH), f32),
                pltpu.VMEM((GROUP, QCONV * DH, DH), bf16),
                pltpu.VMEM((QROWS, DH), jnp.int32),
                pltpu.VMEM((QROWS, DH), jnp.int32),
                pltpu.VMEM((QCONV, ROWS, DH), bf16),
                pltpu.VMEM((GROUP, WINDOWS, QROWS, DH), f32),
                pltpu.VMEM((GROUP, WINDOWS * ROWS, QCONV * DH), bf16),
                pltpu.VMEM((GROUP, WINDOWS, ROWS, DH), f32),
                pltpu.VMEM((GROUP * ROWS, WINDOWS * DH), bf16),
                pltpu.VMEM((GROUP, ROWS, DH), f32),
                pltpu.VMEM((WINDOWS * DH, COLS), bf16),
                pltpu.VMEM((GROUP * ROWS, COLS), f32),
                pltpu.VMEM((ROWS, COLS), bf16),
                pltpu.VMEM((ring_y, ROWS, COLS), bf16),
                pltpu.VMEM((ring_y, ROWS, COLS), bf16),
                pltpu.VMEM((far, ROWS, COLS), bf16),
                pltpu.VMEM((far, ROWS, COLS), bf16),
                pltpu.VMEM((PAD, COLS), bf16),
                pltpu.SemaphoreType.DMA((8,)),
                pltpu.SemaphoreType.DMA((2,)),
                pltpu.SemaphoreType.DMA((2,)),
                pltpu.SemaphoreType.DMA((6, 2 * CHUNKS)),
                pltpu.SemaphoreType.DMA((6, 2 * CHUNKS)),
                pltpu.SemaphoreType.DMA((ring_y,)),
                pltpu.SemaphoreType.DMA((ring_y,)),
                pltpu.SemaphoreType.DMA((far,)),
                pltpu.SemaphoreType.DMA((far,)),
            ],
            compiler_params=pltpu.CompilerParams(
                collective_id=0, has_side_effects=True, vmem_limit_bytes=56 * 1024 * 1024
            ),
        )(
            turn_lengths,
            queries,
            keys,
            values,
            jnp.transpose(theta, (1, 0, 2)),
            mix,
            gain.reshape(1, COLS),
            out_weight,
        )

    return jax.shard_map(
        per_device,
        mesh=mesh,
        in_specs=(
            P("pb", "ha"),
            P("pb", "ha"),
            P("pb", "ha"),
            P("ha", None, None),
            P("ha", None),
            P("ha"),
            P("ha", None),
            P(),
        ),
        out_specs=P("pb", "ha"),
        check_vma=False,
    )
```

```python
import functools
import math

import jax
import jax.numpy as jnp
from jax import lax
from jax.experimental import pallas as pl
from jax.experimental.pallas import tpu as pltpu
from jax.sharding import PartitionSpec as P

GROUP = 4
QCONV = 6
KCONV = 11
REACH = (KCONV - 1) // 2
MAXBACK = 5
ROWS = 128
DH = 128
COLS = GROUP * DH
RING_X = 4
CORES = 2
PAD = 16
STEP = 112
WINDOWS = 7
SPAN = PAD + (MAXBACK + 1) * ROWS + PAD
QROWS = PAD + ROWS
MESH = pl.DeviceIdType.MESH
FOUR, ONE, TWO, THREE, FIVE, TWO_BACK = range(6)
PHASES = ((6, 5, 2, 4, 3), (0, 1))
FAR = 2
CHUNKS = 4
CHUNK = ROWS // CHUNKS
KEY_CHUNKS = tuple(range(CHUNKS))
VALUE_CHUNKS = tuple(range(CHUNKS, 2 * CHUNKS))


def slot_row(distance):
    return PAD + (MAXBACK - distance) * ROWS


def kernel(
    pb_size,
    ha_size,
    turns_hbm,
    q_hbm,
    k_hbm,
    v_hbm,
    theta_hbm,
    mix_hbm,
    gain_hbm,
    w_hbm,
    out_ref,
    turns_ref,
    theta_ref,
    mix_ref,
    gain_ref,
    qext,
    kwin,
    vwin,
    w_vmem,
    taps,
    band,
    row_lo,
    row_hi,
    row_ok,
    shifted,
    lhs,
    conv_buf,
    probs,
    inv_total,
    vext,
    acc,
    normed,
    core_out,
    core_in,
    chip_out,
    chip_in,
    q_behind,
    load_sem,
    tail_send,
    tail_recv,
    send_sem,
    recv_sem,
    core_send,
    core_recv,
    chip_send,
    chip_recv,
):
    pb = lax.axis_index("pb")
    ha = lax.axis_index("ha")
    ring_z = pb_size // RING_X
    ring_y = ha_size // CORES
    x, z = pb % RING_X, pb // RING_X
    core, y = ha % CORES, ha // CORES

    def at(new_z, new_x):
        return ((new_z % ring_z) * RING_X + new_x % RING_X, ha)

    x_next, x_back = at(z, x + 1), at(z, x + RING_X - 1)
    z_next, z_back = at(z + 1, x), at(z + ring_z - 1, x)
    twin = (pb, y * CORES + 1 - core)

    def chip(k):
        return (pb, ((y + k) % ring_y) * CORES + core)

    own = slot_row(0)
    loads = [
        pltpu.make_async_copy(k_hbm, kwin.at[pl.ds(own, ROWS)], load_sem.at[0]),
        pltpu.make_async_copy(v_hbm, vwin.at[pl.ds(own, ROWS)], load_sem.at[1]),
        pltpu.make_async_copy(q_hbm, qext.at[pl.ds(PAD, ROWS)], load_sem.at[2]),
        pltpu.make_async_copy(turns_hbm, turns_ref, load_sem.at[4]),
        pltpu.make_async_copy(theta_hbm, theta_ref, load_sem.at[5]),
        pltpu.make_async_copy(mix_hbm, mix_ref, load_sem.at[6]),
        pltpu.make_async_copy(gain_hbm, gain_ref, load_sem.at[7]),
        pltpu.make_async_copy(w_hbm, w_vmem, load_sem.at[3]),
    ]
    for load in loads:
        load.start()

    barrier = pltpu.get_barrier_semaphore()
    has_next, has_back = z < ring_z - 1, z > 0
    greeted = [x_next, x_back, twin]
    greeted += [chip(k) for k in range(1, ring_y)]

    def greet(other):
        pl.semaphore_signal(barrier, inc=1, device_id=other, device_id_type=MESH)

    for other in greeted:
        greet(other)

    @pl.when(has_next)
    def _():
        greet(z_next)

    @pl.when(has_back)
    def _():
        greet(z_back)

    for win in (kwin, vwin):
        for distance in range(1, MAXBACK + 1):

            @pl.when(pb < distance)
            def _(win=win, row=slot_row(distance)):
                win[row : row + ROWS] = jnp.zeros((ROWS, COLS), jnp.bfloat16)

    @pl.when(pb < 1)
    def _():
        qext[0:PAD] = jnp.zeros((PAD, COLS), jnp.bfloat16)

    pl.semaphore_wait(
        barrier, len(greeted) + has_next.astype(jnp.int32) + has_back.astype(jnp.int32)
    )

    def arrived(kind, chunk):
        distance = {ONE: 1, TWO: 2, THREE: 3, FOUR: 4, FIVE: 5}[kind]

        @pl.when(pb >= distance)
        def _():
            message(kind, chunk).wait_recv()

    def message(kind, chunk):
        win = kwin if chunk < CHUNKS else vwin
        shift = (chunk % CHUNKS) * CHUNK
        behind = slot_row(4)
        src, dst, target = {
            FOUR: (own, slot_row(4), z_next),
            ONE: (jnp.where(x < 3, own, behind), slot_row(1), x_next),
            TWO: (slot_row(1), slot_row(2), x_next),
            THREE: (jnp.where(x < 1, own, behind), slot_row(3), x_back),
            FIVE: (slot_row(1), slot_row(5), z_next),
            TWO_BACK: (slot_row(3), slot_row(2), x_back),
        }[kind]
        return pltpu.make_async_remote_copy(
            src_ref=win.at[pl.ds(pl.multiple_of(src + shift, 16), CHUNK)],
            dst_ref=win.at[pl.ds(dst + shift, CHUNK)],
            send_sem=send_sem.at[kind, chunk],
            recv_sem=recv_sem.at[TWO if kind == TWO_BACK else kind, chunk],
            device_id=target,
            device_id_type=MESH,
        )

    def tail_copy(src, dst, n, target):
        return pltpu.make_async_remote_copy(
            src_ref=src,
            dst_ref=dst,
            send_sem=tail_send.at[n],
            recv_sem=tail_recv.at[n],
            device_id=target,
            device_id_type=MESH,
        )

    tail_z = tail_copy(qext.at[pl.ds(ROWS, PAD)], q_behind, 0, z_next)
    tail_own = tail_copy(qext.at[pl.ds(ROWS, PAD)], qext.at[pl.ds(0, PAD)], 1, x_next)
    tail_behind = tail_copy(q_behind, qext.at[pl.ds(0, PAD)], 1, x_next)

    def steps(chunk):
        return ((ONE, 3), (THREE, 1))

    def from_own(chunk):
        for kind, bound in steps(chunk):

            @pl.when(x < bound)
            def _(kind=kind):
                message(kind, chunk).start()

    def from_behind(chunk):
        arrived(FOUR, chunk)
        for kind, bound in steps(chunk):

            @pl.when((x >= bound) & has_back)
            def _(kind=kind):
                message(kind, chunk).start()

    def to_four(chunk):
        @pl.when(has_next)
        def _():
            message(FOUR, chunk).start()

    def to_five(chunk):
        arrived(ONE, chunk)

        @pl.when(has_next & (pb > 0))
        def _():
            message(FIVE, chunk).start()

    def to_two(chunk):
        @pl.when((x < 3) & (pb > 0))
        def _():
            message(TWO, chunk).start()

    def back_to_two(chunk):
        @pl.when((x == 1) & has_back)
        def _():
            message(THREE, chunk).wait_recv()
            message(TWO_BACK, chunk).start()

    loads[2].wait()

    @pl.when(has_next)
    def _():
        tail_z.start()

    @pl.when(x < 3)
    def _():
        tail_own.start()

    loads[0].wait()
    for chunk in KEY_CHUNKS:
        to_four(chunk)
        from_own(chunk)
    loads[1].wait()
    for chunk in VALUE_CHUNKS:
        to_four(chunk)
    loads[3].wait()
    loads[4].wait()
    first_row = pb * ROWS
    for win in (kwin, vwin):
        win[0:PAD] = jnp.zeros((PAD, COLS), jnp.bfloat16)
        win[SPAN - PAD : SPAN] = jnp.zeros((PAD, COLS), jnp.bfloat16)
    pos = first_row - PAD + lax.broadcasted_iota(jnp.int32, (QROWS, DH), 0)
    row_start = jnp.zeros((QROWS, DH), jnp.int32)
    start = jnp.int32(0)
    for n in range(turns_ref.shape[0]):
        row_start = jnp.where(pos >= start, start, row_start)
        start = start + turns_ref[n]
    key_zero = first_row - slot_row(0)
    row_lo[...] = row_start - key_zero
    row_hi[...] = pos - key_zero
    rel = (pos - row_start)[PAD:]
    for a in range(QCONV):
        row_ok[a] = jnp.where(rel >= a, 1.0, 0.0).astype(jnp.bfloat16)
    taps[...] = jnp.zeros(taps.shape, jnp.float32)
    scaled_theta = theta_ref[...] * (1.0 / math.sqrt(DH))
    taps[:, 0:GROUP, 0 : REACH + 1] = scaled_theta[:, :, REACH:]
    taps[:, 0:GROUP, DH - REACH : DH] = scaled_theta[:, :, :REACH]

    @pl.when(has_back)
    def _():
        tail_z.wait_recv()

    @pl.when((x == 3) & has_back)
    def _():
        tail_behind.start()

    for chunk in KEY_CHUNKS:
        from_behind(chunk)


    for chunk in VALUE_CHUNKS:
        from_own(chunk)

    def make_band(h, carry):
        for a in range(QCONV):
            line = jnp.broadcast_to(taps[a, pl.ds(h, 1), :], (DH, DH))
            square = pltpu.roll(line, 0, 1, stride=1, stride_axis=0)
            band[h, a * DH : (a + 1) * DH, :] = square.astype(jnp.bfloat16)
        return carry

    lax.fori_loop(0, GROUP, make_band, 0)
    for chunk in KEY_CHUNKS:
        to_five(chunk)
        to_two(chunk)
    for chunk in KEY_CHUNKS:
        back_to_two(chunk)

    @pl.when(pb >= 1)
    def _():
        tail_own.wait_recv()

    lane = lax.broadcasted_iota(jnp.int32, (ROWS, DH), 1)
    q_lane = lax.broadcasted_iota(jnp.int32, (QROWS, DH), 1)
    inner = (lane >= 8) & (lane < 8 + STEP)

    def convolve(windows):
        for h in range(GROUP):
            q_head = qext[:, h * DH : (h + 1) * DH]
            for t in windows:
                k_head = kwin[t * STEP : t * STEP + DH, h * DH : (h + 1) * DH]
                scores = lax.dot_general(
                    q_head,
                    k_head,
                    (((1,), (1,)), ((), ())),
                    preferred_element_type=jnp.float32,
                )
                place = q_lane + t * STEP
                seen = (place >= row_lo[...]) & (place <= row_hi[...])
                shifted[h, t] = jnp.where(seen, scores, 0.0)
        for h in range(GROUP):
            for n, t in enumerate(windows):
                for a in range(QCONV):
                    moved = shifted[h, t, PAD - a : PAD - a + ROWS, :].astype(jnp.bfloat16)
                    lhs[h, n * ROWS : (n + 1) * ROWS, a * DH : (a + 1) * DH] = (
                        moved * row_ok[a]
                    )
        lo, hi = row_lo[PAD:], row_hi[PAD:]
        for h in range(GROUP):
            conv = jnp.dot(
                lhs[h, : len(windows) * ROWS], band[h], preferred_element_type=jnp.float32
            )
            for n, t in enumerate(windows):
                place = lane + t * STEP
                kept = (place >= lo) & (place <= hi) & inner
                piece = conv[n * ROWS : (n + 1) * ROWS]
                conv_buf[h, t] = jnp.where(kept, piece, -1e30)

    near, far = range(FAR, WINDOWS), range(FAR)

    for chunk in VALUE_CHUNKS:
        from_behind(chunk)
    for chunk in KEY_CHUNKS:

        @pl.when((pb >= 3) & (x != 1))
        def _(chunk=chunk):
            message(THREE, chunk).wait_recv()

    for chunk in VALUE_CHUNKS:
        to_five(chunk)
        to_two(chunk)
    for chunk in VALUE_CHUNKS:
        back_to_two(chunk)
    for chunk in KEY_CHUNKS:
        arrived(TWO, chunk)
    convolve(PHASES[0])
    for chunk in KEY_CHUNKS:
        arrived(FIVE, chunk)

    convolve(PHASES[1])
    for h in range(GROUP):
        peak = conv_buf[h, 0]
        for t in range(1, WINDOWS):
            peak = jnp.maximum(peak, conv_buf[h, t])
        peak = jnp.max(peak, axis=1, keepdims=True)
        total = jnp.zeros((ROWS, DH), jnp.float32)
        for t in range(WINDOWS):
            weights = jnp.exp(conv_buf[h, t] - peak)
            total = total + weights
            probs[h * ROWS : (h + 1) * ROWS, t * DH : (t + 1) * DH] = weights.astype(
                jnp.bfloat16
            )
        total = jnp.sum(total, axis=1, keepdims=True)
        inv_total[h] = jnp.broadcast_to(1.0 / total, (ROWS, DH))
    split = FAR * DH
    for chunk in VALUE_CHUNKS:
        arrived(TWO, chunk)

        @pl.when((pb >= 3) & (x != 1))
        def _(chunk=chunk):
            message(THREE, chunk).wait_recv()

    for t in near:
        vext[t * DH : (t + 1) * DH] = vwin[t * STEP : t * STEP + DH]

    acc[...] = jnp.dot(probs[:, split:], vext[split:], preferred_element_type=jnp.float32)
    for chunk in VALUE_CHUNKS:
        arrived(FIVE, chunk)
    for t in far:
        vext[t * DH : (t + 1) * DH] = vwin[t * STEP : t * STEP + DH]

    acc[...] += jnp.dot(probs[:, :split], vext[:split], preferred_element_type=jnp.float32)
    for load in loads[5:]:
        load.wait()
    for h in range(GROUP):
        attn = jnp.zeros((ROWS, DH), jnp.float32)
        for p in range(GROUP):
            piece = acc[p * ROWS : (p + 1) * ROWS, h * DH : (h + 1) * DH] * inv_total[p]
            attn = attn + mix_ref[h, p] * piece
        mean_sq = jnp.mean(attn * attn, axis=1, keepdims=True)
        scaled = attn * lax.rsqrt(mean_sq + 1e-06) * gain_ref[:, h * DH : (h + 1) * DH]
        normed[:, h * DH : (h + 1) * DH] = scaled.astype(jnp.bfloat16)

    def partial(k, side):
        group = ((y + k) % ring_y) * CORES + side
        cols = pl.ds(pl.multiple_of(group * COLS, COLS), COLS)
        return jnp.dot(normed[...], w_vmem[:, cols], preferred_element_type=jnp.float32)

    def to_twin(k):
        return pltpu.make_async_remote_copy(
            src_ref=core_out.at[k],
            dst_ref=core_in.at[k],
            send_sem=core_send.at[k],
            recv_sem=core_recv.at[k],
            device_id=twin,
            device_id_type=MESH,
        )

    def to_chip(k):
        return pltpu.make_async_remote_copy(
            src_ref=chip_out.at[k - 1],
            dst_ref=chip_in.at[k - 1],
            send_sem=chip_send.at[k - 1],
            recv_sem=chip_recv.at[k - 1],
            device_id=chip(k),
            device_id_type=MESH,
        )

    order = [1, 3, 2, 0] if ring_y == 4 else list(range(ring_y - 1, -1, -1))
    for k in order:
        core_out[k] = partial(k, 1 - core).astype(jnp.bfloat16)
        to_twin(k).start()
    for k in order:
        mine = partial(k, core).astype(jnp.bfloat16).astype(jnp.float32)
        to_twin(k).wait_recv()
        pair = mine + core_in[k].astype(jnp.float32)
        if k:
            chip_out[k - 1] = pair.astype(jnp.bfloat16)
            to_chip(k).start()
        else:
            acc[0:ROWS] = pair
    result = acc[0:ROWS]
    for k in sorted(order[:-1], key=lambda k: k == 2):
        to_chip(k).wait_recv()
        result = result + chip_in[k - 1].astype(jnp.float32)
    out_ref[...] = result.astype(jnp.bfloat16)

    both = KEY_CHUNKS + VALUE_CHUNKS
    sends = (
        (ONE, (x < 3) | has_back, both),
        (TWO, (x < 3) & (pb > 0), both),
        (TWO_BACK, (x == 1) & has_back, both),
        (THREE, (x < 1) | has_back, both),
        (FOUR, has_next, both),
        (FIVE, has_next & (pb > 0), both),
    )
    for kind, sent, chunks in sends:

        @pl.when(sent)
        def _(kind=kind, chunks=chunks):
            for chunk in chunks:
                message(kind, chunk).wait_send()

    @pl.when(has_next)
    def _():
        tail_z.wait_send()

    @pl.when((x < 3) | has_back)
    def _():
        tail_own.wait_send()

    for k in order:
        to_twin(k).wait_send()
        if k:
            to_chip(k).wait_send()


def solution(mesh):
    pb_size, ha_size = mesh.shape["pb"], mesh.shape["ha"]
    ring_y = ha_size // CORES
    bf16, f32 = jnp.bfloat16, jnp.float32

    def per_device(queries, keys, values, theta, mix, gain, out_weight, turn_lengths):
        hbm = pl.BlockSpec(memory_space=pltpu.HBM)
        vmem = pl.BlockSpec(memory_space=pltpu.VMEM)
        far = max(ring_y - 1, 1)
        return pl.pallas_call(
            functools.partial(kernel, pb_size, ha_size),
            out_shape=jax.ShapeDtypeStruct((ROWS, COLS), bf16),
            in_specs=[hbm] * 8,
            out_specs=vmem,
            scratch_shapes=[
                pltpu.SMEM(turn_lengths.shape, jnp.int32),
                pltpu.VMEM((QCONV, GROUP, KCONV), f32),
                pltpu.SMEM(mix.shape, f32),
                pltpu.VMEM((1, COLS), f32),
                pltpu.VMEM((QROWS, COLS), bf16),
                pltpu.VMEM((SPAN, COLS), bf16),
                pltpu.VMEM((SPAN, COLS), bf16),
                pltpu.VMEM(out_weight.shape, bf16),
                pltpu.VMEM((QCONV, 8, DH), f32),
                pltpu.VMEM((GROUP, QCONV * DH, DH), bf16),
                pltpu.VMEM((QROWS, DH), jnp.int32),
                pltpu.VMEM((QROWS, DH), jnp.int32),
                pltpu.VMEM((QCONV, ROWS, DH), bf16),
                pltpu.VMEM((GROUP, WINDOWS, QROWS, DH), f32),
                pltpu.VMEM((GROUP, WINDOWS * ROWS, QCONV * DH), bf16),
                pltpu.VMEM((GROUP, WINDOWS, ROWS, DH), f32),
                pltpu.VMEM((GROUP * ROWS, WINDOWS * DH), bf16),
                pltpu.VMEM((GROUP, ROWS, DH), f32),
                pltpu.VMEM((WINDOWS * DH, COLS), bf16),
                pltpu.VMEM((GROUP * ROWS, COLS), f32),
                pltpu.VMEM((ROWS, COLS), bf16),
                pltpu.VMEM((ring_y, ROWS, COLS), bf16),
                pltpu.VMEM((ring_y, ROWS, COLS), bf16),
                pltpu.VMEM((far, ROWS, COLS), bf16),
                pltpu.VMEM((far, ROWS, COLS), bf16),
                pltpu.VMEM((PAD, COLS), bf16),
                pltpu.SemaphoreType.DMA((8,)),
                pltpu.SemaphoreType.DMA((2,)),
                pltpu.SemaphoreType.DMA((2,)),
                pltpu.SemaphoreType.DMA((6, 2 * CHUNKS)),
                pltpu.SemaphoreType.DMA((6, 2 * CHUNKS)),
                pltpu.SemaphoreType.DMA((ring_y,)),
                pltpu.SemaphoreType.DMA((ring_y,)),
                pltpu.SemaphoreType.DMA((far,)),
                pltpu.SemaphoreType.DMA((far,)),
            ],
            compiler_params=pltpu.CompilerParams(
                collective_id=0, has_side_effects=True, vmem_limit_bytes=56 * 1024 * 1024
            ),
        )(
            turn_lengths,
            queries,
            keys,
            values,
            jnp.transpose(theta, (1, 0, 2)),
            mix,
            gain.reshape(1, COLS),
            out_weight,
        )

    return jax.shard_map(
        per_device,
        mesh=mesh,
        in_specs=(
            P("pb", "ha"),
            P("pb", "ha"),
            P("pb", "ha"),
            P("ha", None, None),
            P("ha", None),
            P("ha"),
            P("ha", None),
            P(),
        ),
        out_specs=P("pb", "ha"),
        check_vma=False,
    )
```
